32 devices in a mesh: elem: 8 (over z, y), face: 4 (over x, core).
Axes of the slice: x: 2, y: 2, z: 4, core: 2. Of those that a mesh axis runs over, the one named last changes fastest.
Arguments:
- vol_inverse: bfloat16 [128, 320, 320], P(('elem', 'face')), may hold values from -0.3125 to 0.3125
- vol_from_trace: bfloat16 [128, 320, 480], P(('elem', 'face')), may hold values from -0.25 to 0.25
- trace_from_vol: bfloat16 [128, 480, 320], P(('elem', 'face')), may hold values from -0.25 to 0.25
- vol_residual: bfloat16 [128, 320], P(('elem', 'face')), may hold values from -6 to 6
- face_ids: int32 [128, 6], P(('elem', 'face')), may hold values from 0 to 383, as said below
- trace_residual: float32 [384, 80], P(('elem', 'face')), may hold values from -6 to 6
- stabilization: float32 [384, 80], P(('elem', 'face')), may hold values from 1.5 to 4
Outputs:
- trace_update: float32 [384, 80], P(('elem', 'face'))
- vol_update: float32 [128, 320], P(('elem', 'face'))
The draws below stay inside these ranges and needn't reach their ends.
Inputs may be any that keep to these rules, and one draw needn't show every extreme that they name: `face_ids`: owner group g holds elements g * 16 to (g + 1) * 16 - 1 and faces g * 48 to (g + 1) * 48 - 1. Every face is named by exactly two slots, and the 6 slots of one element name different faces. The slots of group g name faces of group g, or faces 0 to 15 of group (g - 1) mod 8; faces 0 to 15 of group g are named by one slot of group g and one slot of group (g + 1) mod 8; all other faces of group g are named by two slots of group g.
All inputs are finite; a program needn't handle non-finite values.
Results may differ from the reference program's by a relative error of at most 0.007.
Values may be sent and summed in bfloat16 or wider, within the bound.
No kernel may reach another device: no remote copies, remote signals or barrier semaphores. Data moves between devices by JAX's collectives and lax.ppermute only.
A program may use at most 64 MiB of HBM per device.

```python
import math
import jax
import jax.numpy as jnp
from jax import lax

V = 320
W = 80
SIDES = 6
SWEEPS = 5
TRACE = 480
GROUPS = 8
E_GRP = 16
IFACE = 16
F_GRP = 48
ELEMS = 128
FACES = 384


def group_slots(key, group_index):
    keys = jax.random.split(key, 4)
    elem_order = jax.random.permutation(keys[0], E_GRP).astype(jnp.int32)
    face_order = jax.random.permutation(keys[1], 2 * E_GRP).astype(jnp.int32)
    side_order = jax.random.permutation(keys[2], 2 * E_GRP).astype(jnp.int32)
    offset_step = jax.random.randint(keys[3], (), 1, E_GRP).astype(jnp.int32)
    places = jnp.arange(2 * E_GRP, dtype=jnp.int32)
    pair_index = places // 2
    column = places % 2
    base = group_index * F_GRP
    inner_ids = base + IFACE + face_order
    first_elem = elem_order[pair_index]
    second_elem = elem_order[(pair_index + offset_step) % E_GRP]
    lower_base = (group_index + GROUPS - 1) % GROUPS * F_GRP
    rim_ids = jnp.where(side_order < IFACE, base + side_order, lower_base + side_order - IFACE)
    table = jnp.zeros((E_GRP, SIDES), jnp.int32)
    table = table.at[first_elem, column].set(inner_ids)
    table = table.at[second_elem, column + 2].set(inner_ids)
    table = table.at[pair_index, column + 4].set(rim_ids)
    return table


def draw_face_ids(key, part):
    keys = jax.random.split(jax.random.fold_in(key, 17), GROUPS)
    tables = jax.vmap(group_slots)(keys, jnp.arange(GROUPS, dtype=jnp.int32))
    return tables.reshape(ELEMS, SIDES).astype(jnp.int32)


def levels(stream_key, extent, cuts, least, largest):
    def one(axis_at, parts):
        steps = jax.random.uniform(jax.random.fold_in(jax.random.fold_in(stream_key, 6), axis_at), (parts,), jnp.float32, least / len(cuts), largest / len(cuts))
        return jnp.repeat(jnp.exp(steps), extent[axis_at] // parts).reshape((-1,) + (1,) * (len(extent) - axis_at - 1))

    gain = one(*cuts[0])
    for cut in cuts[1:]:
        gain = gain * one(*cut)
    return gain


def scatter_about(stream_key, dims, spread, most, pieces=(), kind=jnp.bfloat16):
    entries = spread * jax.random.normal(stream_key, dims, jnp.float32)
    if pieces:
        entries = entries * levels(stream_key, dims, pieces, -0.22, 0.18)
    return jnp.clip(entries, -most, most).astype(kind)


def setup_inputs(seed: int = 0) -> dict:
    key_list = jax.random.split(jax.random.key(seed), 8)
    return {
        "vol_inverse": scatter_about(key_list[0], (ELEMS, V, V), V ** -0.5, 0.3125, ((0, 32),)),
        "vol_from_trace": scatter_about(key_list[1], (ELEMS, V, TRACE), TRACE ** -0.5, 0.25, ((0, 32),)),
        "trace_from_vol": scatter_about(key_list[2], (ELEMS, TRACE, V), (2 * V) ** -0.5, 0.25, ((0, 32),)),
        "vol_residual": scatter_about(key_list[3], (ELEMS, V), 1.0, 6.0, ((0, 32),)),
        "face_ids": draw_face_ids(jax.random.fold_in(key_list[7], 71), 0),
        "trace_residual": scatter_about(key_list[5], (FACES, W), 1.0, 6.0, ((0, 32),), jnp.float32),
        "stabilization": jnp.clip(jnp.exp(math.log(4.0) - 0.98082925 * jax.random.uniform(key_list[6], (FACES, W), jnp.float32) ** levels(key_list[6], (FACES, W), ((0, 32),), -0.2, 0.2)), 1.5, 4.0),
    }


def reference(vol_inverse, vol_from_trace, trace_from_vol, vol_residual, face_ids, trace_residual, stabilization):
    face_total, trace_width = trace_residual.shape
    elem_total = vol_inverse.shape[0]
    slot_faces = face_ids.reshape(elem_total * SIDES).astype(jnp.int32)

    def first_pass(blocks):
        inverse, from_vol, residual = blocks
        local_row = jnp.dot(inverse, residual, preferred_element_type=jnp.float32)
        load_row = jnp.dot(from_vol, local_row.astype(jnp.bfloat16), preferred_element_type=jnp.float32)
        return local_row, load_row

    local_part, trace_load = lax.map(first_pass, (vol_inverse, trace_from_vol, vol_residual))

    def assemble(terms):
        return jax.ops.segment_sum(terms.reshape(elem_total * SIDES, trace_width), slot_faces, num_segments=face_total)

    def to_slots(trace_rows):
        return trace_rows.astype(jnp.bfloat16)[slot_faces].reshape(elem_total, SIDES * trace_width)

    right_side = trace_residual - assemble(trace_load)
    trace_now = right_side / stabilization

    def image_pass(blocks):
        inverse, up_block, from_vol, lam_row = blocks
        couple = jnp.dot(inverse, up_block, preferred_element_type=jnp.float32).astype(jnp.bfloat16)
        schur_block = jnp.dot(from_vol, couple, preferred_element_type=jnp.float32).astype(jnp.bfloat16)
        return jnp.dot(schur_block, lam_row, preferred_element_type=jnp.float32)

    for sweep_index in range(SWEEPS - 1):
        lam_elem = to_slots(trace_now)
        image_terms = lax.map(image_pass, (vol_inverse, vol_from_trace, trace_from_vol, lam_elem))
        trace_now = (right_side + assemble(image_terms)) / stabilization

    lam_elem = to_slots(trace_now)

    def back_pass(blocks):
        inverse, up_block, local_row, lam_row = blocks
        couple = jnp.dot(inverse, up_block, preferred_element_type=jnp.float32).astype(jnp.bfloat16)
        return local_row - jnp.dot(couple, lam_row, preferred_element_type=jnp.float32)

    vol_update = lax.map(back_pass, (vol_inverse, vol_from_trace, local_part, lam_elem))
    return trace_now, vol_update
```

```python
import jax
import jax.numpy as jnp
from jax import lax
from jax.sharding import PartitionSpec as P

SWEEPS = 5
AXES = ("elem", "face")
CORES = 2


def partners(groups, chips, offset, shifts):
    route = []
    for group in range(groups):
        side = 1 if (group - offset) % 2 == 0 else -1
        other = (group + side) % groups
        for chip in range(chips):
            for core in range(CORES):
                target = (chip + side * shifts[core]) % chips
                route.append(
                    (
                        (group * chips + chip) * CORES + core,
                        (other * chips + target) * CORES + core,
                    )
                )
    return route


def along_x(groups, chips, shift):
    return [
        (
            (group * chips + chip) * CORES + core,
            (group * chips + (chip + shift) % chips) * CORES + (core + 1) % CORES,
        )
        for group in range(groups)
        for chip in range(chips)
        for core in range(CORES)
    ]


def other_core(groups, chips):
    count = groups * chips
    return [(chip * CORES + core, chip * CORES + 1 - core) for chip in range(count) for core in range(CORES)]


def local(
    vol_inverse,
    vol_from_trace,
    trace_from_vol,
    vol_residual,
    face_ids,
    trace_residual,
    stabilization,
):
    groups = lax.axis_size("elem")
    members = lax.axis_size("face")
    chips = members // CORES
    elem_count, side_count = face_ids.shape
    own_faces, width = trace_residual.shape
    group_faces = own_faces * members
    border = elem_count * members
    rows = group_faces + border
    group_index = lax.axis_index("elem")
    member = lax.axis_index("face")
    lower_group = (group_index + groups - 1) % groups
    even = group_index % 2 == 0

    def swap_core(block):
        return lax.ppermute(block, AXES, other_core(groups, chips))

    def total(part):
        first, last = part[:border], part[group_faces:]
        to_first = jnp.where(even, first, last)
        to_second = jnp.where(even, last, first)
        from_second = from_first = 0.0
        for shift in range(0, chips, CORES):
            shifts = [shift + core for core in range(CORES)]
            got = lax.ppermute(to_second, AXES, partners(groups, chips, 1, shifts))
            from_second = from_second + got + swap_core(got)
        for shift in range(0, chips, CORES):
            shifts = [shift + core for core in range(CORES)]
            got = lax.ppermute(to_first, AXES, partners(groups, chips, 0, shifts))
            from_first = from_first + got + swap_core(got)
        own = part
        for shift in range(1, chips):
            own = own + lax.ppermute(part, AXES, along_x(groups, chips, shift))
        upper = jnp.where(even, from_first, from_second)
        lower = jnp.where(even, from_second, from_first)
        return jnp.concatenate(
            [own[:border] + upper, own[border:group_faces], own[group_faces:] + lower], axis=0
        )

    def row_of(ids):
        own = ids - group_index * group_faces
        low = ids - lower_group * group_faces
        inside = (own >= 0) & (own < group_faces)
        return jnp.where(inside, own, low + group_faces)

    own_rows = row_of(face_ids)
    own_hits = (
        own_rows.reshape(-1)[:, None] == lax.broadcasted_iota(jnp.int32, (1, rows), 1)
    ).astype(jnp.float32)

    local_part = jnp.einsum(
        "evk,ek->ev", vol_inverse, vol_residual, preferred_element_type=jnp.float32
    )
    trace_load = jnp.einsum(
        "etv,ev->et",
        trace_from_vol,
        local_part.astype(jnp.bfloat16),
        preferred_element_type=jnp.float32,
    )
    load_sums = jnp.einsum(
        "sf,sw->fw", own_hits, trace_load.reshape(-1, width), precision=lax.Precision.HIGHEST
    )
    blank = jnp.zeros((rows, width), jnp.float32)
    place = member * own_faces
    residual_rows = lax.dynamic_update_slice(blank, trace_residual, (place, 0))
    stab_rows = lax.dynamic_update_slice(blank, stabilization, (place, 0))
    slots = elem_count * side_count
    id_column = jnp.pad(own_rows.reshape(slots, 1).astype(jnp.float32), ((0, rows - slots), (0, 0)))
    packet = jnp.concatenate([residual_rows - load_sums, stab_rows, id_column], axis=1)
    mate = swap_core(packet)
    first_total = total((packet + mate)[:, : 2 * width])
    mate_rows = mate[:slots, 2 * width].astype(jnp.int32)
    hits = jnp.concatenate([own_rows.reshape(-1), mate_rows])[:, None] == lax.broadcasted_iota(
        jnp.int32, (1, rows), 1
    )
    hits_half = hits.astype(jnp.bfloat16)
    hits_float = hits.astype(jnp.float32)

    couple = jnp.einsum(
        "evk,ekt->evt", vol_inverse, vol_from_trace, preferred_element_type=jnp.float32
    ).astype(jnp.bfloat16)
    schur_own = jnp.einsum(
        "etv,evs->ets", trace_from_vol, couple, preferred_element_type=jnp.float32
    ).astype(jnp.bfloat16)
    schur_mate = swap_core(schur_own)

    right_side = first_total[:, :width]
    inverse_stab = 1.0 / first_total[:, width:]

    def gather(trace_now):
        values = jnp.dot(hits_half, trace_now.astype(jnp.bfloat16), preferred_element_type=jnp.float32)
        return values.astype(jnp.bfloat16).reshape(2 * elem_count, side_count * width)

    trace_now = right_side * inverse_stab
    for _ in range(SWEEPS - 1):
        lam = gather(trace_now)
        image = jnp.concatenate(
            [
                jnp.einsum("ets,es->et", block, part, preferred_element_type=jnp.float32)
                for block, part in ((schur_own, lam[:elem_count]), (schur_mate, lam[elem_count:]))
            ]
        )
        image_sums = jnp.einsum(
            "sf,sw->fw", hits_float, image.reshape(-1, width), precision=lax.Precision.HIGHEST
        )
        trace_now = (right_side + total(image_sums)) * inverse_stab
    lam = gather(trace_now)[:elem_count]
    vol_update = local_part - jnp.einsum(
        "evt,et->ev", couple, lam, preferred_element_type=jnp.float32
    )
    return lax.dynamic_slice_in_dim(trace_now, place, own_faces, 0), vol_update


def solution(mesh):
    in_specs = (
        P(AXES, None, None),
        P(AXES, None, None),
        P(AXES, None, None),
        P(AXES, None),
        P(AXES, None),
        P(AXES, None),
        P(AXES, None),
    )
    out_specs = (P(AXES, None), P(AXES, None))
    return jax.shard_map(local, mesh=mesh, in_specs=in_specs, out_specs=out_specs, check_vma=False)
```

```python
import functools

import jax
import jax.numpy as jnp
from jax import lax
from jax.experimental import pallas as pl
from jax.experimental.pallas import tpu as pltpu
from jax.sharding import PartitionSpec as P

SWEEPS = 5
AXES = ("elem", "face")
CORES = 2
F32 = jnp.float32
HALF = jnp.bfloat16
VMEM = pl.BlockSpec(memory_space=pltpu.VMEM)
HBM = pl.BlockSpec(memory_space=pltpu.HBM)


def partners(groups, chips, offset, shifts):
    route = []
    for group in range(groups):
        side = 1 if (group - offset) % 2 == 0 else -1
        other = (group + side) % groups
        for chip in range(chips):
            for core in range(CORES):
                target = (chip + side * shifts[core]) % chips
                route.append(
                    (
                        (group * chips + chip) * CORES + core,
                        (other * chips + target) * CORES + core,
                    )
                )
    return route


def along_x(groups, chips, shift):
    return [
        (
            (group * chips + chip) * CORES + core,
            (group * chips + (chip + shift) % chips) * CORES + (core + 1) % CORES,
        )
        for group in range(groups)
        for chip in range(chips)
        for core in range(CORES)
    ]


def other_core(groups, chips):
    return [
        (chip * CORES + core, chip * CORES + 1 - core)
        for chip in range(groups * chips)
        for core in range(CORES)
    ]


def call(body, shapes, *args, limit=16, stay=0, scratch=()):
    outs = [jax.ShapeDtypeStruct(shape, kind) for shape, kind in shapes]
    args = [
        pltpu.with_memory_space_constraint(arg, pltpu.HBM) if n < stay else arg
        for n, arg in enumerate(args)
    ]
    return pl.pallas_call(
        body,
        out_shape=outs,
        in_specs=[HBM] * stay + [VMEM] * (len(args) - stay),
        out_specs=[VMEM] * len(outs),
        scratch_shapes=list(scratch),
        compiler_params=pltpu.CompilerParams(vmem_limit_bytes=limit * 2**20),
    )(*args)


def fetch(sources, targets, sems):
    copies = [
        [
            pltpu.make_async_copy(source.at[e], target.at[e], sems.at[n, e])
            for e in range(source.shape[0])
        ]
        for n, (source, target) in enumerate(zip(sources, targets))
    ]
    for row in zip(*copies):
        for copy in row:
            copy.start()
    return copies


def contract(left, right, left_dim, right_dim):
    return lax.dot_general(
        left, right, (((left_dim,), (right_dim,)), ((), ())), preferred_element_type=F32
    )


def add_up(refs):
    value = refs[0][...]
    for ref in refs[1:]:
        value = value + ref[...]
    return value


def to_lanes(rows, elems, sides):
    return jnp.concatenate([rows[elems * k : elems * (k + 1)] for k in range(sides)], axis=1)


def to_rows(lanes, sides, width):
    return jnp.concatenate([lanes[:, width * k : width * (k + 1)] for k in range(sides)], axis=0)


def spread(spread_hits, values):
    high = values.astype(HALF)
    low = (values - high.astype(F32)).astype(HALF)
    return contract(spread_hits, high, 1, 0) + contract(spread_hits, low, 1, 0)


def hit_rows(ids, rows, group_faces, border, groups):
    group = lax.axis_index("elem")
    own = ids - group * group_faces
    low = ids - lax.rem(group + groups - 1, groups) * group_faces
    place = jnp.where((own >= 0) & (own < group_faces), own, low + group_faces)
    place = jnp.where(ids < 0, -1, place)
    elems, sides = ids.shape
    lane = lax.broadcasted_iota(jnp.int32, (elems, rows), 1)
    return jnp.concatenate(
        [(place[:, k : k + 1] == lane).astype(F32) for k in range(sides)], axis=0
    )


def masked(rows, element):
    index = lax.broadcasted_iota(jnp.int32, rows.shape, 0)
    return jnp.where(index == element, rows, 0.0).astype(HALF)


def load_kernel(dims, *refs):
    groups, elems, sides, width, group_faces, border = dims
    big, small, (local_ref, packet_ref, ids_ref, inverse, down) = refs[:2], refs[2:6], refs[6:11]
    residual, ids, residual_rows, stab_rows, big_sems, small_sems = refs[11:]
    rows = group_faces + border
    lines = 2 * elems
    smalls = [
        pltpu.make_async_copy(source, target, small_sems.at[n])
        for n, (source, target) in enumerate(zip(small, (residual, ids, residual_rows, stab_rows)))
    ]
    for copy in smalls:
        copy.start()
    inverse_copies, down_copies = fetch(big, (inverse, down), big_sems)
    for copy in smalls:
        copy.wait()
    ids_ref[...] = jnp.full((lines, sides), -1, jnp.int32)
    ids_ref[:elems] = ids[...]
    hits = hit_rows(ids_ref[...], rows, group_faces, border, groups)
    spread_hits = hits.T.astype(HALF)
    own_faces = residual_rows.shape[0]
    place = lax.axis_index("face") * own_faces
    blank = jnp.zeros((rows - own_faces, width), F32)
    right = pltpu.roll(jnp.concatenate([residual_rows[...], blank], axis=0), place, 0)
    scale = pltpu.roll(jnp.concatenate([stab_rows[...], blank], axis=0), place, 0)
    packet_ref[:lines, 2 * width :] = ids_ref[...].astype(F32)
    local_ref[...] = jnp.zeros(local_ref.shape, F32)
    source = jnp.concatenate([residual[...].astype(F32), jnp.zeros((elems, residual.shape[1]), F32)], axis=0)
    load = None
    for e in range(elems):
        inverse_copies[e].wait()
        local = contract(masked(source, e), inverse[e], 1, 1)
        local_ref[...] += local
        down_copies[e].wait()
        part = contract(local.astype(HALF), down[e], 1, 0)
        load = part if load is None else load + part
    sums = spread(spread_hits, to_rows(load, sides, width))
    packet_ref[:, : 2 * width] = jnp.concatenate([right - sums, scale], axis=1)


def join_kernel(border, width, packet, mate, sums_ref, first_ref, second_ref):
    sums = packet[:, : 2 * width] + mate[:, : 2 * width]
    sums_ref[...] = sums
    deal(sums, border, first_ref, second_ref)


def deal(sums, border, first_ref, second_ref):
    even = lax.rem(lax.axis_index("elem"), 2) == 0
    upper, lower = sums[:border], sums[sums.shape[0] - border :]
    first_ref[...] = jnp.where(even, upper, lower)
    second_ref[:border] = jnp.where(even, lower, upper)
    second_ref[border:] = first_ref[...]


def hits_kernel(dims, ids, mate, hits_ref, spread_ref):
    groups, elems, sides, width, group_faces, border = dims
    far = mate[:elems, 2 * width :].astype(jnp.int32)
    both = jnp.concatenate([ids[:elems], far], axis=0)
    hits = hit_rows(both, group_faces + border, group_faces, border, groups)
    hits_ref[...] = hits.astype(HALF)
    spread_ref[...] = hits.T.astype(HALF)


def whole(own, first, second, border):
    even = lax.rem(lax.axis_index("elem"), 2) == 0
    a, b = add_up(first), add_up(second)[:border]
    upper, lower = jnp.where(even, a, b), jnp.where(even, b, a)
    sums = add_up(own)
    last = sums.shape[0] - border
    return jnp.concatenate([sums[:border] + upper, sums[border:last], sums[last:] + lower], axis=0)


def image(trace_now, hits, spread_hits, schur_own, schur_mate, sides):
    elems = schur_own.shape[0]
    width = trace_now.shape[1]
    picked = contract(hits[...], trace_now.astype(HALF), 1, 0)
    lam = to_lanes(picked, 2 * elems, sides)
    terms = None
    for e in range(2 * elems):
        block = schur_own[e] if e < elems else schur_mate[e - elems]
        part = contract(masked(lam, e), block, 1, 0)
        terms = part if terms is None else terms + part
    return spread(spread_hits[...], to_rows(terms, sides, width))


def first_kernel(counts, border, sides, *refs):
    own, first, second, rest = split(counts, refs)
    hits, spread_hits, schur_own, schur_mate, right_ref, scale_ref, sums_ref, first_ref, second_ref = rest
    both = whole(own, first, second, border)
    width = both.shape[1] // 2
    right = both[:, :width]
    scale = 1.0 / both[:, width:]
    right_ref[...] = right
    scale_ref[...] = scale
    sums = image(right * scale, hits, spread_hits, schur_own, schur_mate, sides)
    sums_ref[...] = sums
    deal(sums, border, first_ref, second_ref)


def step_kernel(counts, border, sides, *refs):
    own, first, second, rest = split(counts, refs)
    right, scale, hits, spread_hits, schur_own, schur_mate, sums_ref, first_ref, second_ref = rest
    trace_now = (whole(own, first, second, border) + right[...]) * scale[...]
    sums = image(trace_now, hits, spread_hits, schur_own, schur_mate, sides)
    sums_ref[...] = sums
    deal(sums, border, first_ref, second_ref)


def last_kernel(counts, border, sides, *refs):
    own, first, second, rest = split(counts, refs)
    right, scale, hits, couple, local, trace_ref, vol_ref = rest
    trace_now = (whole(own, first, second, border) + right[...]) * scale[...]
    own_faces = trace_ref.shape[0]
    place = lax.axis_index("face") * own_faces
    rows = trace_now.shape[0]
    trace_ref[...] = pltpu.roll(trace_now, lax.rem(rows - place, rows), 0)[:own_faces]
    elems = couple.shape[0]
    picked = contract(hits[...], trace_now.astype(HALF), 1, 0)
    lam = to_lanes(picked, 2 * elems, sides)
    value = local[...]
    for e in range(elems):
        value = value - contract(masked(lam, e), couple[e], 1, 1)
    vol_ref[...] = value[:elems]


def split(counts, refs):
    a, b, c = counts
    return refs[:a], refs[a : a + b], refs[a + b : a + b + c], refs[a + b + c :]


def local(
    vol_inverse,
    vol_from_trace,
    trace_from_vol,
    vol_residual,
    face_ids,
    trace_residual,
    stabilization,
):
    groups = lax.axis_size("elem")
    members = lax.axis_size("face")
    chips = members // CORES
    elems, sides = face_ids.shape
    volume = vol_residual.shape[1]
    own_faces, width = trace_residual.shape
    group_faces = own_faces * members
    border = elems * members
    rows = group_faces + border
    slots = 2 * elems * sides
    trace = sides * width
    dims = (groups, elems, sides, width, group_faces, border)

    def swap_core(block):
        return lax.ppermute(block, AXES, other_core(groups, chips))

    def exchange(part, to_first, to_second):
        straight = [
            [shift + core for core in range(CORES)] for shift in range(0, chips, CORES)
        ]
        second = [lax.ppermute(to_second, AXES, partners(groups, chips, 1, s)) for s in straight]
        first = [lax.ppermute(to_first, AXES, partners(groups, chips, 0, s)) for s in straight]
        own = [part] + [
            lax.ppermute(part, AXES, along_x(groups, chips, shift)) for shift in range(1, chips)
        ]
        first = first + [swap_core(block) for block in first]
        second = second + [swap_core(block) for block in second]
        return own, first, second

    down = jnp.swapaxes(trace_from_vol, 1, 2)
    large = (vol_inverse, down)
    small = (vol_residual, face_ids, trace_residual, stabilization)
    local_part, packet, ids, inverse, down = call(
        functools.partial(load_kernel, dims),
        [
            ((2 * elems, volume), F32),
            ((rows, 2 * width + sides), F32),
            ((2 * elems, sides), jnp.int32),
            *((array.shape, array.dtype) for array in large),
        ],
        *large, *small,
        stay=6,
        scratch=[
            *(pltpu.VMEM(array.shape, array.dtype) for array in small),
            pltpu.SemaphoreType.DMA((len(large), elems)),
            pltpu.SemaphoreType.DMA((len(small),)),
        ],
    )
    mate = swap_core(packet)
    couple = jnp.einsum(
        "evk,ekt->evt", inverse, vol_from_trace, preferred_element_type=F32
    ).astype(HALF)
    schur_own = jnp.einsum("evs,evt->est", couple, down, preferred_element_type=F32).astype(HALF)
    mate, schur_own = lax.optimization_barrier((mate, schur_own))
    schur_mate = swap_core(schur_own)
    sums, to_first, to_second = call(
        functools.partial(join_kernel, border, width),
        [((rows, 2 * width), F32), ((border, 2 * width), F32), ((2 * border, 2 * width), F32)],
        packet, mate,
    )
    hits, spread_hits = call(
        functools.partial(hits_kernel, dims),
        [((slots, rows), HALF), ((rows, slots), HALF)],
        ids, mate,
    )

    def counted(kernel, parts):
        return functools.partial(kernel, tuple(len(part) for part in parts), border, sides)

    def flat(parts):
        return [ref for part in parts for ref in part]

    dealt = [((rows, width), F32), ((border, width), F32), ((2 * border, width), F32)]
    parts = exchange(sums, to_first, to_second)
    right, scale, *out = call(
        counted(first_kernel, parts),
        [((rows, width), F32)] * 2 + dealt,
        *flat(parts), hits, spread_hits, schur_own, schur_mate,
    )
    for _ in range(SWEEPS - 2):
        parts = exchange(*out)
        out = call(
            counted(step_kernel, parts), dealt,
            *flat(parts), right, scale, hits, spread_hits, schur_own, schur_mate,
        )
    parts = exchange(*out)
    trace_update, vol_update = call(
        counted(last_kernel, parts),
        [((own_faces, width), F32), ((elems, volume), F32)],
        *flat(parts), right, scale, hits, couple, local_part,
    )
    return trace_update, vol_update


def solution(mesh):
    in_specs = (
        P(AXES, None, None),
        P(AXES, None, None),
        P(AXES, None, None),
        P(AXES, None),
        P(AXES, None),
        P(AXES, None),
        P(AXES, None),
    )
    out_specs = (P(AXES, None), P(AXES, None))
    return jax.shard_map(local, mesh=mesh, in_specs=in_specs, out_specs=out_specs, check_vma=False)
```

```python
import functools

import jax
import jax.numpy as jnp
from jax import lax
from jax.experimental import pallas as pl
from jax.experimental.pallas import tpu as pltpu
from jax.sharding import PartitionSpec as P

SWEEPS = 5
AXES = ("elem", "face")
CORES = 2
F32 = jnp.float32
HALF = jnp.bfloat16
VMEM = pl.BlockSpec(memory_space=pltpu.VMEM)
HBM = pl.BlockSpec(memory_space=pltpu.HBM)


def partners(groups, chips, offset, shifts):
    route = []
    for group in range(groups):
        side = 1 if (group - offset) % 2 == 0 else -1
        other = (group + side) % groups
        for chip in range(chips):
            for core in range(CORES):
                target = (chip + side * shifts[core]) % chips
                route.append(
                    (
                        (group * chips + chip) * CORES + core,
                        (other * chips + target) * CORES + core,
                    )
                )
    return route


def along_x(groups, chips, shift):
    return [
        (
            (group * chips + chip) * CORES + core,
            (group * chips + (chip + shift) % chips) * CORES + (core + 1) % CORES,
        )
        for group in range(groups)
        for chip in range(chips)
        for core in range(CORES)
    ]


def other_core(groups, chips):
    return [
        (chip * CORES + core, chip * CORES + 1 - core)
        for chip in range(groups * chips)
        for core in range(CORES)
    ]


def call(body, shapes, *args, limit=16, stay=0, scratch=()):
    outs = [jax.ShapeDtypeStruct(shape, kind) for shape, kind in shapes]
    args = [
        pltpu.with_memory_space_constraint(arg, pltpu.HBM) if n < stay else arg
        for n, arg in enumerate(args)
    ]
    return pl.pallas_call(
        body,
        out_shape=outs,
        in_specs=[HBM] * stay + [VMEM] * (len(args) - stay),
        out_specs=[VMEM] * len(outs),
        scratch_shapes=list(scratch),
        compiler_params=pltpu.CompilerParams(vmem_limit_bytes=limit * 2**20),
    )(*args)


def contract(left, right, left_dim, right_dim):
    return lax.dot_general(
        left, right, (((left_dim,), (right_dim,)), ((), ())), preferred_element_type=F32
    )


def add_up(refs):
    value = refs[0][...].astype(F32)
    for ref in refs[1:]:
        value = value + ref[...].astype(F32)
    return value


def to_lanes(rows, elems, sides):
    return jnp.concatenate([rows[elems * k : elems * (k + 1)] for k in range(sides)], axis=1)


def to_rows(lanes, sides, width):
    return jnp.concatenate([lanes[:, width * k : width * (k + 1)] for k in range(sides)], axis=0)


def spread(spread_hits, values):
    high = values.astype(HALF)
    low = (values - high.astype(F32)).astype(HALF)
    return contract(spread_hits, high, 1, 0) + contract(spread_hits, low, 1, 0)


def hit_rows(ids, rows, group_faces, border, groups):
    group = lax.axis_index("elem")
    own = ids - group * group_faces
    low = ids - lax.rem(group + groups - 1, groups) * group_faces
    place = jnp.where((own >= 0) & (own < group_faces), own, low + group_faces)
    place = jnp.where(ids < 0, -1, place)
    elems, sides = ids.shape
    lane = lax.broadcasted_iota(jnp.int32, (elems, rows), 1)
    return jnp.concatenate(
        [(place[:, k : k + 1] == lane).astype(F32) for k in range(sides)], axis=0
    )


def masked(rows, element):
    index = lax.broadcasted_iota(jnp.int32, rows.shape, 0)
    return jnp.where(index == element, rows, 0.0).astype(HALF)


def load_kernel(dims, *refs):
    groups, elems, sides, width, group_faces, border = dims
    sources, (local_ref, packet_ref, ids_ref, inverse, down) = refs[:6], refs[6:11]
    residual, ids, residual_rows, stab_rows, sems = refs[11:]
    rows = group_faces + border
    lines = 2 * elems

    def fetch(index, target, at, count, sem):
        piece = pl.ds(at, count)
        copy = pltpu.make_async_copy(sources[index].at[piece], target.at[piece], sems.at[sem])
        copy.start()
        return copy

    inverse_hbm, down_hbm, residual_hbm, ids_hbm, residual_rows_hbm, stab_rows_hbm = range(6)
    own_faces = residual_rows.shape[0]
    first = [fetch(residual_hbm, residual, 0, elems, 0), fetch(inverse_hbm, inverse, 0, elems, 1)]
    half = elems // 1
    pieces = [fetch(down_hbm, down, half * n, half, 2 + n) for n in range(1)]
    small = [
        fetch(ids_hbm, ids, 0, elems, 2 + 1),
        fetch(residual_rows_hbm, residual_rows, 0, own_faces, 3 + 1),
        fetch(stab_rows_hbm, stab_rows, 0, own_faces, 4 + 1),
    ]
    for copy in first:
        copy.wait()
    source = residual[...].astype(F32)
    source = jnp.concatenate([source, jnp.zeros_like(source)], axis=0)
    local = add_up([contract(masked(source, e), inverse[e], 1, 1) for e in range(elems)])
    local_ref[...] = local
    for copy in small:
        copy.wait()
    ids_ref[...] = jnp.full((lines, sides), -1, jnp.int32)
    ids_ref[:elems] = ids[...]
    hits = hit_rows(ids_ref[...], rows, group_faces, border, groups)
    spread_hits = hits.T.astype(HALF)
    place = lax.axis_index("face") * own_faces
    blank = jnp.zeros((rows - own_faces, width), F32)
    right = pltpu.roll(jnp.concatenate([residual_rows[...], blank], axis=0), place, 0)
    scale = pltpu.roll(jnp.concatenate([stab_rows[...], blank], axis=0), place, 0)
    packet_ref[:lines, 2 * width :] = ids_ref[...].astype(F32)
    load = []
    for n in range(1):
        pieces[n].wait()
        for e in range(half * n, half * (n + 1)):
            load.append(contract(masked(local, e), down[e], 1, 0))
    sums = spread(spread_hits, to_rows(add_up(load), sides, width))
    packet_ref[:, : 2 * width] = jnp.concatenate([right - sums, scale], axis=1)


def join_kernel(border, width, packet, mate, sums_ref, first_ref, second_ref):
    sums = packet[:, : 2 * width] + mate[:, : 2 * width]
    sums_ref[...] = sums
    deal(sums, border, first_ref, second_ref)


def deal(sums, border, first_ref, second_ref):
    even = lax.rem(lax.axis_index("elem"), 2) == 0
    upper, lower = sums[:border], sums[sums.shape[0] - border :]
    kind = first_ref.dtype
    first_ref[...] = jnp.where(even, upper, lower).astype(kind)
    second_ref[:border] = jnp.where(even, lower, upper).astype(kind)
    second_ref[border:] = first_ref[: second_ref.shape[0] - border]


def hits_kernel(dims, ids, mate, hits_ref, spread_ref):
    groups, elems, sides, width, group_faces, border = dims
    far = mate[:elems, 2 * width :].astype(jnp.int32)
    both = jnp.concatenate([ids[:elems], far], axis=0)
    hits = hit_rows(both, group_faces + border, group_faces, border, groups)
    hits_ref[...] = hits.astype(HALF)
    spread_ref[...] = hits.T.astype(HALF)


def whole(parts, border):
    own, first, second, (mate,) = parts
    even = lax.rem(lax.axis_index("elem"), 2) == 0
    blocks = mate[...].astype(F32)
    a, b = add_up(first), add_up(second)[:border]
    for n in range(len(first)):
        a = a + blocks[n * border : (n + 1) * border]
        b = b + blocks[(len(first) + n) * border : (len(first) + n + 1) * border]
    upper, lower = jnp.where(even, a, b), jnp.where(even, b, a)
    sums = add_up(own)
    last = sums.shape[0] - border
    return jnp.concatenate([sums[:border] + upper, sums[border:last], sums[last:] + lower], axis=0)


def image(trace_now, hits, spread_hits, schur_own, schur_mate, sides):
    elems = schur_own.shape[0]
    width = trace_now.shape[1]
    picked = contract(hits[...], trace_now.astype(HALF), 1, 0)
    lam = to_lanes(picked, 2 * elems, sides)
    terms = None
    for e in range(2 * elems):
        block = schur_own[e] if e < elems else schur_mate[e - elems]
        part = contract(masked(lam, e), block, 1, 0)
        terms = part if terms is None else terms + part
    return spread(spread_hits[...], to_rows(terms, sides, width))


def first_kernel(counts, border, sides, *refs):
    parts, rest = split(counts, refs)
    hits, spread_hits, schur_own, schur_mate, right_ref, scale_ref, sums_ref, sent_ref, first_ref, second_ref = rest
    both = whole(parts, border)
    width = both.shape[1] // 2
    right = both[:, :width]
    scale = 1.0 / both[:, width:]
    right_ref[...] = right
    scale_ref[...] = scale
    sums = image(right * scale, hits, spread_hits, schur_own, schur_mate, sides)
    sums_ref[...] = sums
    sent_ref[...] = sums.astype(HALF)
    deal(sums, border, first_ref, second_ref)


def step_kernel(counts, border, sides, *refs):
    parts, rest = split(counts, refs)
    right, scale, hits, spread_hits, schur_own, schur_mate, sums_ref, sent_ref, first_ref, second_ref = rest
    trace_now = (whole(parts, border) + right[...]) * scale[...]
    sums = image(trace_now, hits, spread_hits, schur_own, schur_mate, sides)
    sums_ref[...] = sums
    sent_ref[...] = sums.astype(HALF)
    deal(sums, border, first_ref, second_ref)


def last_kernel(counts, border, sides, *refs):
    parts, rest = split(counts, refs)
    right, scale, hits, couple, local, trace_ref, vol_ref = rest
    trace_now = (whole(parts, border) + right[...]) * scale[...]
    own_faces = trace_ref.shape[0]
    place = lax.axis_index("face") * own_faces
    rows = trace_now.shape[0]
    trace_ref[...] = pltpu.roll(trace_now, lax.rem(rows - place, rows), 0)[:own_faces]
    elems = couple.shape[0]
    picked = contract(hits[...], trace_now.astype(HALF), 1, 0)
    lam = to_lanes(picked, 2 * elems, sides)
    value = local[...]
    for e in range(elems):
        value = value - contract(masked(lam, e), couple[e], 1, 1)
    vol_ref[...] = value[:elems]


def split(counts, refs):
    parts = []
    for count in counts:
        parts.append(refs[:count])
        refs = refs[count:]
    return parts, refs


def local(
    vol_inverse,
    vol_from_trace,
    trace_from_vol,
    vol_residual,
    face_ids,
    trace_residual,
    stabilization,
):
    groups = lax.axis_size("elem")
    members = lax.axis_size("face")
    chips = members // CORES
    elems, sides = face_ids.shape
    volume = vol_residual.shape[1]
    own_faces, width = trace_residual.shape
    group_faces = own_faces * members
    border = elems * members
    rows = group_faces + border
    slots = 2 * elems * sides
    trace = sides * width
    dims = (groups, elems, sides, width, group_faces, border)

    def swap_core(block):
        return lax.ppermute(block, AXES, other_core(groups, chips))

    def exchange(part, sent, to_first, to_second):
        straight = [
            [shift + core for core in range(CORES)] for shift in range(0, chips, CORES)
        ]
        second = [lax.ppermute(to_second, AXES, partners(groups, chips, 1, s)) for s in straight]
        first = [lax.ppermute(to_first, AXES, partners(groups, chips, 0, s)) for s in straight]
        own = [part] + [
            lax.ppermute(sent, AXES, along_x(groups, chips, shift)) for shift in range(1, chips)
        ]
        mate = swap_core(jnp.concatenate([*first, *(block[:border] for block in second)]))
        return own, first, second, [mate]

    down = jnp.swapaxes(trace_from_vol, 1, 2)
    large = (vol_inverse, down)
    small = (vol_residual, face_ids, trace_residual, stabilization)
    local_part, packet, ids, inverse, down = call(
        functools.partial(load_kernel, dims),
        [
            ((2 * elems, volume), F32),
            ((rows, 2 * width + sides), F32),
            ((2 * elems, sides), jnp.int32),
            *((array.shape, array.dtype) for array in large),
        ],
        *large, *small,
        stay=6,
        scratch=[
            *(pltpu.VMEM(array.shape, array.dtype) for array in small),
            pltpu.SemaphoreType.DMA((6,)),
        ],
    )
    mate = swap_core(packet)
    couple = jnp.einsum(
        "evk,ekt->evt", inverse, vol_from_trace, preferred_element_type=F32
    ).astype(HALF)
    schur_own = jnp.einsum("evs,evt->est", couple, down, preferred_element_type=F32).astype(HALF)
    mate, schur_own = lax.optimization_barrier((mate, schur_own))
    schur_mate = swap_core(schur_own)
    sums, to_first, to_second = call(
        functools.partial(join_kernel, border, width),
        [((rows, 2 * width), F32), ((border, 2 * width), F32), ((border + 8, 2 * width), F32)],
        packet, mate,
    )
    hits, spread_hits = call(
        functools.partial(hits_kernel, dims),
        [((slots, rows), HALF), ((rows, slots), HALF)],
        ids, mate,
    )

    def counted(kernel, parts):
        return functools.partial(kernel, tuple(len(part) for part in parts), border, sides)

    def flat(parts):
        return [ref for part in parts for ref in part]

    dealt = [
        ((rows, width), F32),
        ((rows, width), HALF),
        ((border, width), HALF),
        ((2 * border, width), HALF),
    ]
    parts = exchange(sums, sums, to_first, to_second)
    right, scale, *out = call(
        counted(first_kernel, parts),
        [((rows, width), F32)] * 2 + dealt,
        *flat(parts), hits, spread_hits, schur_own, schur_mate,
    )
    for _ in range(SWEEPS - 2):
        parts = exchange(*out)
        out = call(
            counted(step_kernel, parts), dealt,
            *flat(parts), right, scale, hits, spread_hits, schur_own, schur_mate,
        )
    parts = exchange(*out)
    trace_update, vol_update = call(
        counted(last_kernel, parts),
        [((own_faces, width), F32), ((elems, volume), F32)],
        *flat(parts), right, scale, hits, couple, local_part,
    )
    return trace_update, vol_update


def solution(mesh):
    in_specs = (
        P(AXES, None, None),
        P(AXES, None, None),
        P(AXES, None, None),
        P(AXES, None),
        P(AXES, None),
        P(AXES, None),
        P(AXES, None),
    )
    out_specs = (P(AXES, None), P(AXES, None))
    return jax.shard_map(local, mesh=mesh, in_specs=in_specs, out_specs=out_specs, check_vma=False)
```

```python
import functools

import jax
import jax.numpy as jnp
from jax import lax
from jax.experimental import pallas as pl
from jax.experimental.pallas import tpu as pltpu
from jax.sharding import PartitionSpec as P

SWEEPS = 5
AXES = ("elem", "face")
CORES = 2
F32 = jnp.float32
HALF = jnp.bfloat16
VMEM = pl.BlockSpec(memory_space=pltpu.VMEM)
HBM = pl.BlockSpec(memory_space=pltpu.HBM)


def partners(groups, chips, offset, shifts):
    route = []
    for group in range(groups):
        side = 1 if (group - offset) % 2 == 0 else -1
        other = (group + side) % groups
        for chip in range(chips):
            for core in range(CORES):
                target = (chip + side * shifts[core]) % chips
                route.append(
                    (
                        (group * chips + chip) * CORES + core,
                        (other * chips + target) * CORES + core,
                    )
                )
    return route


def along_x(groups, chips, shift):
    return [
        (
            (group * chips + chip) * CORES + core,
            (group * chips + (chip + shift) % chips) * CORES + (core + 1) % CORES,
        )
        for group in range(groups)
        for chip in range(chips)
        for core in range(CORES)
    ]


def other_core(groups, chips):
    return [
        (chip * CORES + core, chip * CORES + 1 - core)
        for chip in range(groups * chips)
        for core in range(CORES)
    ]


def call(body, shapes, *args, limit=16, stay=0, scratch=(), cost=None):
    outs = [jax.ShapeDtypeStruct(shape, kind) for shape, kind in shapes]
    args = [
        pltpu.with_memory_space_constraint(arg, pltpu.HBM) if n < stay else arg
        for n, arg in enumerate(args)
    ]
    return pl.pallas_call(
        body,
        out_shape=outs,
        in_specs=[HBM] * stay + [VMEM] * (len(args) - stay),
        out_specs=[VMEM] * len(outs),
        scratch_shapes=list(scratch),
        cost_estimate=cost,
        compiler_params=pltpu.CompilerParams(vmem_limit_bytes=limit * 2**20),
    )(*args)


def contract(left, right, left_dim, right_dim):
    return lax.dot_general(
        left, right, (((left_dim,), (right_dim,)), ((), ())), preferred_element_type=F32
    )


def add_up(refs):
    value = refs[0][...].astype(F32)
    for ref in refs[1:]:
        value = value + ref[...].astype(F32)
    return value


def to_lanes(rows, elems, sides):
    return jnp.concatenate([rows[elems * k : elems * (k + 1)] for k in range(sides)], axis=1)


def to_rows(lanes, sides, width):
    return jnp.concatenate([lanes[:, width * k : width * (k + 1)] for k in range(sides)], axis=0)


def spread(spread_hits, values):
    high = values.astype(HALF)
    low = (values - high.astype(F32)).astype(HALF)
    return contract(spread_hits, high, 1, 0) + contract(spread_hits, low, 1, 0)


def hit_rows(ids, rows, group_faces, border, groups):
    group = lax.axis_index("elem")
    own = ids - group * group_faces
    low = ids - lax.rem(group + groups - 1, groups) * group_faces
    place = jnp.where((own >= 0) & (own < group_faces), own, low + group_faces)
    place = jnp.where(ids < 0, -1, place)
    elems, sides = ids.shape
    lane = lax.broadcasted_iota(jnp.int32, (elems, rows), 1)
    return jnp.concatenate(
        [(place[:, k : k + 1] == lane).astype(F32) for k in range(sides)], axis=0
    )


def masked(rows, element):
    index = lax.broadcasted_iota(jnp.int32, rows.shape, 0)
    return jnp.where(index == element, rows, 0.0).astype(HALF)


def load_kernel(dims, *refs):
    groups, elems, sides, width, group_faces, border = dims
    sources, (local_ref, packet_ref, ids_ref, inverse, down) = refs[:6], refs[6:11]
    residual, ids, residual_rows, stab_rows, sems = refs[11:]
    rows = group_faces + border
    lines = 2 * elems

    def fetch(index, target, at, count, sem):
        piece = pl.ds(at, count)
        copy = pltpu.make_async_copy(sources[index].at[piece], target.at[piece], sems.at[sem])
        copy.start()
        return copy

    inverse_hbm, down_hbm, residual_hbm, ids_hbm, residual_rows_hbm, stab_rows_hbm = range(6)
    own_faces = residual_rows.shape[0]
    first = [fetch(residual_hbm, residual, 0, elems, 0), fetch(inverse_hbm, inverse, 0, elems, 1)]
    half = elems // 1
    pieces = [fetch(down_hbm, down, half * n, half, 2 + n) for n in range(1)]
    small = [
        fetch(ids_hbm, ids, 0, elems, 2 + 1),
        fetch(residual_rows_hbm, residual_rows, 0, own_faces, 3 + 1),
        fetch(stab_rows_hbm, stab_rows, 0, own_faces, 4 + 1),
    ]
    for copy in first:
        copy.wait()
    source = residual[...].astype(F32)
    source = jnp.concatenate([source, jnp.zeros_like(source)], axis=0)
    local = add_up([contract(masked(source, e), inverse[e], 1, 1) for e in range(elems)])
    local_ref[...] = local
    for copy in small:
        copy.wait()
    ids_ref[...] = jnp.full((lines, sides), -1, jnp.int32)
    ids_ref[:elems] = ids[...]
    hits = hit_rows(ids_ref[...], rows, group_faces, border, groups)
    spread_hits = hits.T.astype(HALF)
    place = lax.axis_index("face") * own_faces
    blank = jnp.zeros((rows - own_faces, width), F32)
    right = pltpu.roll(jnp.concatenate([residual_rows[...], blank], axis=0), place, 0)
    scale = pltpu.roll(jnp.concatenate([stab_rows[...], blank], axis=0), place, 0)
    packet_ref[:lines, 2 * width :] = ids_ref[...].astype(F32)
    load = []
    for n in range(1):
        pieces[n].wait()
        for e in range(half * n, half * (n + 1)):
            load.append(contract(masked(local, e), down[e], 1, 0))
    sums = spread(spread_hits, to_rows(add_up(load), sides, width))
    packet_ref[:, : 2 * width] = jnp.concatenate([right - sums, scale], axis=1)


def join_kernel(border, width, chip_faces, packet, mate, sums_ref, sent_ref, first_ref, second_ref):
    sums = packet[:, : 2 * width] + mate[:, : 2 * width]
    sums_ref[...] = sums
    half = width // 2
    chip = lax.axis_index("face") // CORES
    scale = pltpu.roll(sums[:, width:], back(chip * chip_faces, sums.shape[0]), 0)[:chip_faces]
    sent_ref[...] = jnp.zeros(sent_ref.shape, F32)
    sent_ref[:, :width] = sums[:, :width]
    sent_ref[:chip_faces, width:] = scale[:, :half]
    sent_ref[chip_faces : 2 * chip_faces, width:] = scale[:, half:]
    deal(sums, border, first_ref, second_ref)


def back(shift, rows):
    return lax.rem(rows - shift, rows)


def deal(sums, border, first_ref, second_ref):
    even = lax.rem(lax.axis_index("elem"), 2) == 0
    upper, lower = sums[:border], sums[sums.shape[0] - border :]
    kind = first_ref.dtype
    first_ref[...] = jnp.where(even, upper, lower).astype(kind)
    second_ref[:border] = jnp.where(even, lower, upper).astype(kind)
    second_ref[border:] = first_ref[: second_ref.shape[0] - border]


def hits_kernel(dims, ids, mate, hits_ref, spread_ref):
    groups, elems, sides, width, group_faces, border = dims
    far = mate[:elems, 2 * width :].astype(jnp.int32)
    both = jnp.concatenate([ids[:elems], far], axis=0)
    hits = hit_rows(both, group_faces + border, group_faces, border, groups)
    hits_ref[...] = hits.astype(HALF)
    spread_ref[...] = hits.T.astype(HALF)


def whole(parts, border):
    own, first, second, (mate,) = parts
    even = lax.rem(lax.axis_index("elem"), 2) == 0
    blocks = mate[...].astype(F32)
    a, b = add_up(first), add_up(second)[:border]
    for n in range(len(first)):
        a = a + blocks[n * border : (n + 1) * border]
        b = b + blocks[(len(first) + n) * border : (len(first) + n + 1) * border]
    upper, lower = jnp.where(even, a, b), jnp.where(even, b, a)
    sums = add_up(own)
    last = sums.shape[0] - border
    return jnp.concatenate([sums[:border] + upper, sums[border:last], sums[last:] + lower], axis=0)


def image(trace_now, hits, spread_hits, schur, sides):
    pieces = [block[e] for block in schur for e in range(block.shape[0])]
    picked = contract(hits[...], trace_now.astype(HALF), 1, 0)
    lam = to_lanes(picked, len(pieces), sides)
    terms = add_up([contract(masked(lam, e), block, 1, 0) for e, block in enumerate(pieces)])
    return spread(spread_hits[...], to_rows(terms, sides, trace_now.shape[1]))


def own_kernel(chip_faces, sums, *refs):
    *across, total_ref = refs
    rows, width = sums.shape[0], sums.shape[1] // 2
    chip = lax.axis_index("face") // CORES
    chips = len(across) + 1
    total = sums[...]
    for n, block in enumerate(across):
        packed = block[...]
        pair = [packed[chip_faces * k : chip_faces * (k + 1), width:] for k in range(2)]
        scale = jnp.concatenate(pair, axis=1)
        scale = jnp.concatenate([scale, jnp.zeros((rows - chip_faces, width), F32)], axis=0)
        scale = pltpu.roll(scale, lax.rem(chip + chips - n - 1, chips) * chip_faces, 0)
        total = total + jnp.concatenate([packed[:, :width], scale], axis=1)
    total_ref[...] = total


def first_kernel(counts, border, sides, *refs):
    parts, rest = split(counts, refs)
    hits, spread_hits, *schur, right_ref, scale_ref, sums_ref, sent_ref, first_ref, second_ref = rest
    both = whole(parts, border)
    width = both.shape[1] // 2
    right = both[:, :width]
    scale = 1.0 / both[:, width:]
    right_ref[...] = right
    scale_ref[...] = scale
    sums = image(right * scale, hits, spread_hits, schur, sides)
    sums_ref[...] = sums
    sent_ref[...] = sums.astype(HALF)
    deal(sums, border, first_ref, second_ref)


def step_kernel(counts, border, sides, *refs):
    parts, rest = split(counts, refs)
    right, scale, hits, spread_hits, *schur, sums_ref, sent_ref, first_ref, second_ref = rest
    trace_now = (whole(parts, border) + right[...]) * scale[...]
    sums = image(trace_now, hits, spread_hits, schur, sides)
    sums_ref[...] = sums
    sent_ref[...] = sums.astype(HALF)
    deal(sums, border, first_ref, second_ref)


def last_kernel(counts, border, sides, *refs):
    parts, rest = split(counts, refs)
    right, scale, hits, couple, local, trace_ref, vol_ref = rest
    trace_now = (whole(parts, border) + right[...]) * scale[...]
    own_faces = trace_ref.shape[0]
    place = lax.axis_index("face") * own_faces
    rows = trace_now.shape[0]
    trace_ref[...] = pltpu.roll(trace_now, back(place, rows), 0)[:own_faces]
    elems = couple.shape[0]
    picked = contract(hits[...], trace_now.astype(HALF), 1, 0)
    lam = to_lanes(picked, 2 * elems, sides)
    value = local[...]
    for e in range(elems):
        value = value - contract(masked(lam, e), couple[e], 1, 1)
    vol_ref[...] = value[:elems]


def split(counts, refs):
    parts = []
    for count in counts:
        parts.append(refs[:count])
        refs = refs[count:]
    return parts, refs


def local(
    vol_inverse,
    vol_from_trace,
    trace_from_vol,
    vol_residual,
    face_ids,
    trace_residual,
    stabilization,
):
    groups = lax.axis_size("elem")
    members = lax.axis_size("face")
    chips = members // CORES
    elems, sides = face_ids.shape
    volume = vol_residual.shape[1]
    own_faces, width = trace_residual.shape
    group_faces = own_faces * members
    border = elems * members
    rows = group_faces + border
    slots = 2 * elems * sides
    trace = sides * width
    dims = (groups, elems, sides, width, group_faces, border)

    def swap_core(block):
        return lax.ppermute(block, AXES, other_core(groups, chips))

    def exchange(part, sent, to_first, to_second):
        straight = [
            [shift + core for core in range(CORES)] for shift in range(0, chips, CORES)
        ]
        second = [lax.ppermute(to_second, AXES, partners(groups, chips, 1, s)) for s in straight]
        first = [lax.ppermute(to_first, AXES, partners(groups, chips, 0, s)) for s in straight]
        own = [part] + [
            lax.ppermute(sent, AXES, along_x(groups, chips, shift)) for shift in range(1, chips)
        ]
        mate = swap_core(jnp.concatenate([*first, *(block[:border] for block in second)]))
        return own, first, second, [mate]

    down = jnp.swapaxes(trace_from_vol, 1, 2)
    large = (vol_inverse, down)
    small = (vol_residual, face_ids, trace_residual, stabilization)
    local_part, packet, ids, inverse, down = call(
        functools.partial(load_kernel, dims),
        [
            ((2 * elems, volume), F32),
            ((rows, 2 * width + sides), F32),
            ((2 * elems, sides), jnp.int32),
            *((array.shape, array.dtype) for array in large),
        ],
        *large, *small,
        stay=6,
        scratch=[
            *(pltpu.VMEM(array.shape, array.dtype) for array in small),
            pltpu.SemaphoreType.DMA((6,)),
        ],
    )
    mate = swap_core(packet)
    couple = jnp.einsum(
        "evk,ekt->evt", inverse, vol_from_trace, preferred_element_type=F32
    ).astype(HALF)
    couple, mate = lax.optimization_barrier((couple, mate))
    chip_faces = CORES * own_faces
    sums, sent, to_first, to_second = call(
        functools.partial(join_kernel, border, width, chip_faces),
        [
            ((rows, 2 * width), F32),
            ((rows, width + width // 2), F32),
            ((border, 2 * width), F32),
            ((border + 8, 2 * width), F32),
        ],
        packet, mate,
    )
    couple, sent = lax.optimization_barrier((couple, sent))
    schur_own = jnp.einsum("evs,evt->est", couple, down, preferred_element_type=F32).astype(HALF)
    schur_mate = swap_core(schur_own)
    hits, spread_hits = call(
        functools.partial(hits_kernel, dims),
        [((slots, rows), HALF), ((rows, slots), HALF)],
        ids, mate,
        cost=pl.CostEstimate(flops=70000000000, bytes_accessed=0, transcendentals=0),
    )

    def counted(kernel, parts):
        return functools.partial(kernel, tuple(len(part) for part in parts), border, sides)

    def flat(parts):
        return [ref for part in parts for ref in part]

    dealt = [
        ((rows, width), F32),
        ((rows, width), HALF),
        ((border, width), HALF),
        ((2 * border, width), HALF),
    ]
    sent, schur_own = lax.optimization_barrier((sent, schur_own))
    (_, *across), *rest = exchange(sums, sent, to_first, to_second)
    own = call(
        functools.partial(own_kernel, chip_faces), [((rows, 2 * width), F32)], sums, *across
    )
    parts = own, *rest
    right, scale, *out = call(
        counted(first_kernel, parts),
        [((rows, width), F32)] * 2 + dealt,
        *flat(parts), hits, spread_hits, schur_own, schur_mate,
    )
    for _ in range(SWEEPS - 2):
        parts = exchange(*out)
        out = call(
            counted(step_kernel, parts), dealt,
            *flat(parts), right, scale, hits, spread_hits, schur_own, schur_mate,
        )
    parts = exchange(*out)
    trace_update, vol_update = call(
        counted(last_kernel, parts),
        [((own_faces, width), F32), ((elems, volume), F32)],
        *flat(parts), right, scale, hits, couple, local_part,
    )
    return trace_update, vol_update


def solution(mesh):
    in_specs = (
        P(AXES, None, None),
        P(AXES, None, None),
        P(AXES, None, None),
        P(AXES, None),
        P(AXES, None),
        P(AXES, None),
        P(AXES, None),
    )
    out_specs = (P(AXES, None), P(AXES, None))
    return jax.shard_map(local, mesh=mesh, in_specs=in_specs, out_specs=out_specs, check_vma=False)
```

```python
import functools

import jax
import jax.numpy as jnp
from jax import lax
from jax.experimental import pallas as pl
from jax.experimental.pallas import tpu as pltpu
from jax.sharding import PartitionSpec as P

SWEEPS = 5
AXES = ("elem", "face")
CORES = 2
F32 = jnp.float32
HALF = jnp.bfloat16
VMEM = pl.BlockSpec(memory_space=pltpu.VMEM)
HBM = pl.BlockSpec(memory_space=pltpu.HBM)


def partners(groups, chips, offset, shifts):
    route = []
    for group in range(groups):
        side = 1 if (group - offset) % 2 == 0 else -1
        other = (group + side) % groups
        for chip in range(chips):
            for core in range(CORES):
                target = (chip + side * shifts[core]) % chips
                route.append(
                    (
                        (group * chips + chip) * CORES + core,
                        (other * chips + target) * CORES + core,
                    )
                )
    return route


def along_x(groups, chips, shift):
    return [
        (
            (group * chips + chip) * CORES + core,
            (group * chips + (chip + shift) % chips) * CORES + (core + 1) % CORES,
        )
        for group in range(groups)
        for chip in range(chips)
        for core in range(CORES)
    ]


def other_core(groups, chips):
    return [
        (chip * CORES + core, chip * CORES + 1 - core)
        for chip in range(groups * chips)
        for core in range(CORES)
    ]


def call(body, shapes, *args, limit=16, stay=0, scratch=(), cost=None):
    outs = [jax.ShapeDtypeStruct(shape, kind) for shape, kind in shapes]
    args = [
        pltpu.with_memory_space_constraint(arg, pltpu.HBM) if n < stay else arg
        for n, arg in enumerate(args)
    ]
    return pl.pallas_call(
        body,
        out_shape=outs,
        in_specs=[HBM] * stay + [VMEM] * (len(args) - stay),
        out_specs=[VMEM] * len(outs),
        scratch_shapes=list(scratch),
        cost_estimate=cost,
        compiler_params=pltpu.CompilerParams(vmem_limit_bytes=limit * 2**20),
    )(*args)


def contract(left, right, left_dim, right_dim):
    return lax.dot_general(
        left, right, (((left_dim,), (right_dim,)), ((), ())), preferred_element_type=F32
    )


def add_up(refs):
    value = refs[0][...].astype(F32)
    for ref in refs[1:]:
        value = value + ref[...].astype(F32)
    return value


def to_lanes(rows, elems, sides):
    return jnp.concatenate([rows[elems * k : elems * (k + 1)] for k in range(sides)], axis=1)


def to_rows(lanes, sides, width):
    return jnp.concatenate([lanes[:, width * k : width * (k + 1)] for k in range(sides)], axis=0)


def spread(spread_hits, values):
    high = values.astype(HALF)
    low = (values - high.astype(F32)).astype(HALF)
    return contract(spread_hits, high, 1, 0) + contract(spread_hits, low, 1, 0)


def hit_rows(ids, rows, group_faces, border, groups):
    group = lax.axis_index("elem")
    own = ids - group * group_faces
    low = ids - lax.rem(group + groups - 1, groups) * group_faces
    place = jnp.where((own >= 0) & (own < group_faces), own, low + group_faces)
    place = jnp.where(ids < 0, -1, place)
    elems, sides = ids.shape
    lane = lax.broadcasted_iota(jnp.int32, (elems, rows), 1)
    return jnp.concatenate(
        [(place[:, k : k + 1] == lane).astype(F32) for k in range(sides)], axis=0
    )


def masked(rows, element):
    index = lax.broadcasted_iota(jnp.int32, rows.shape, 0)
    return jnp.where(index == element, rows, 0.0).astype(HALF)


def load_kernel(dims, *refs):
    groups, elems, sides, width, group_faces, border = dims
    sources, (local_ref, packet_ref, ids_ref, inverse, down) = refs[:6], refs[6:11]
    residual, ids, residual_rows, stab_rows, sems = refs[11:]
    rows = group_faces + border
    lines = 2 * elems

    def fetch(index, target, at, count, sem):
        piece = pl.ds(at, count)
        copy = pltpu.make_async_copy(sources[index].at[piece], target.at[piece], sems.at[sem])
        copy.start()
        return copy

    inverse_hbm, down_hbm, residual_hbm, ids_hbm, residual_rows_hbm, stab_rows_hbm = range(6)
    own_faces = residual_rows.shape[0]
    first = [fetch(residual_hbm, residual, 0, elems, 0), fetch(inverse_hbm, inverse, 0, elems, 1)]
    half = elems // 1
    pieces = [fetch(down_hbm, down, half * n, half, 2 + n) for n in range(1)]
    small = [
        fetch(ids_hbm, ids, 0, elems, 2 + 1),
        fetch(residual_rows_hbm, residual_rows, 0, own_faces, 3 + 1),
        fetch(stab_rows_hbm, stab_rows, 0, own_faces, 4 + 1),
    ]
    for copy in first:
        copy.wait()
    source = residual[...].astype(F32)
    source = jnp.concatenate([source, jnp.zeros_like(source)], axis=0)
    local = add_up([contract(masked(source, e), inverse[e], 1, 1) for e in range(elems)])
    local_ref[...] = local
    for copy in small:
        copy.wait()
    ids_ref[...] = jnp.full((lines, sides), -1, jnp.int32)
    ids_ref[:elems] = ids[...]
    hits = hit_rows(ids_ref[...], rows, group_faces, border, groups)
    spread_hits = hits.T.astype(HALF)
    place = lax.axis_index("face") * own_faces
    blank = jnp.zeros((rows - own_faces, width), F32)
    right = pltpu.roll(jnp.concatenate([residual_rows[...], blank], axis=0), place, 0)
    scale = pltpu.roll(jnp.concatenate([stab_rows[...], blank], axis=0), place, 0)
    packet_ref[:lines, 2 * width :] = ids_ref[...].astype(F32)
    load = []
    for n in range(1):
        pieces[n].wait()
        for e in range(half * n, half * (n + 1)):
            load.append(contract(masked(local, e), down[e], 1, 0))
    sums = spread(spread_hits, to_rows(add_up(load), sides, width))
    packet_ref[:, : 2 * width] = jnp.concatenate([right - sums, scale], axis=1)


def join_kernel(border, width, packet, mate, sums_ref, first_ref, second_ref):
    sums = packet[:, : 2 * width] + mate[:, : 2 * width]
    sums_ref[...] = sums
    deal(sums, border, first_ref, second_ref)


def pack_kernel(chip_faces, sums, sent_ref):
    width = sums.shape[1] // 2
    half = width // 2
    chip = lax.axis_index("face") // CORES
    scale = pltpu.roll(sums[:, width:], back(chip * chip_faces, sums.shape[0]), 0)[:chip_faces]
    sent_ref[...] = jnp.zeros(sent_ref.shape, F32)
    sent_ref[:, :width] = sums[:, :width]
    sent_ref[:chip_faces, width:] = scale[:, :half]
    sent_ref[chip_faces : 2 * chip_faces, width:] = scale[:, half:]


def back(shift, rows):
    return lax.rem(rows - shift, rows)


def deal(sums, border, first_ref, second_ref):
    even = lax.rem(lax.axis_index("elem"), 2) == 0
    upper, lower = sums[:border], sums[sums.shape[0] - border :]
    kind = first_ref.dtype
    first_ref[:border] = jnp.where(even, upper, lower).astype(kind)
    if first_ref.shape[0] > border:
        first_ref[border:] = sums[: first_ref.shape[0] - border].astype(kind)
    second_ref[:border] = jnp.where(even, lower, upper).astype(kind)
    if second_ref.shape[0] > border:
        second_ref[border:] = sums[: second_ref.shape[0] - border].astype(kind)


def hits_kernel(dims, ids, mate, hits_ref, spread_ref):
    groups, elems, sides, width, group_faces, border = dims
    far = mate[:elems, 2 * width :].astype(jnp.int32)
    both = jnp.concatenate([ids[:elems], far], axis=0)
    hits = hit_rows(both, group_faces + border, group_faces, border, groups)
    hits_ref[...] = hits.astype(HALF)
    spread_ref[...] = hits.T.astype(HALF)


def whole(parts, border):
    own, first, second, (mate,) = parts
    even = lax.rem(lax.axis_index("elem"), 2) == 0
    blocks = mate[...].astype(F32)
    a, b = add_up(first)[:border], add_up(second)[:border]
    for n in range(len(first)):
        a = a + blocks[n * border : (n + 1) * border]
        b = b + blocks[(len(first) + n) * border : (len(first) + n + 1) * border]
    upper, lower = jnp.where(even, a, b), jnp.where(even, b, a)
    sums = add_up(own)
    last = sums.shape[0] - border
    return jnp.concatenate([sums[:border] + upper, sums[border:last], sums[last:] + lower], axis=0)


def image(trace_now, hits, spread_hits, schur, sides):
    pieces = [block[e] for block in schur for e in range(block.shape[0])]
    picked = contract(hits[...], trace_now.astype(HALF), 1, 0)
    lam = to_lanes(picked, len(pieces), sides)
    terms = add_up([contract(masked(lam, e), block, 1, 0) for e, block in enumerate(pieces)])
    return spread(spread_hits[...], to_rows(terms, sides, trace_now.shape[1]))


def own_kernel(chip_faces, sums, *refs):
    *across, total_ref = refs
    rows, width = sums.shape[0], sums.shape[1] // 2
    chip = lax.axis_index("face") // CORES
    chips = len(across) + 1
    total = sums[...]
    for n, block in enumerate(across):
        packed = block[...]
        pair = [packed[chip_faces * k : chip_faces * (k + 1), width:] for k in range(2)]
        scale = jnp.concatenate(pair, axis=1)
        scale = jnp.concatenate([scale, jnp.zeros((rows - chip_faces, width), F32)], axis=0)
        scale = pltpu.roll(scale, lax.rem(chip + chips - n - 1, chips) * chip_faces, 0)
        total = total + jnp.concatenate([packed[:, :width], scale], axis=1)
    total_ref[...] = total


def first_kernel(counts, border, sides, *refs):
    parts, rest = split(counts, refs)
    hits, spread_hits, *schur, right_ref, scale_ref, sums_ref, sent_ref, first_ref, second_ref = rest
    both = whole(parts, border)
    width = both.shape[1] // 2
    right = both[:, :width]
    scale = 1.0 / both[:, width:]
    right_ref[...] = right
    scale_ref[...] = scale
    sums = image(right * scale, hits, spread_hits, schur, sides)
    sums_ref[...] = sums
    sent_ref[...] = sums.astype(HALF)
    deal(sums, border, first_ref, second_ref)


def step_kernel(counts, border, sides, *refs):
    parts, rest = split(counts, refs)
    right, scale, hits, spread_hits, *schur, sums_ref, sent_ref, first_ref, second_ref = rest
    trace_now = (whole(parts, border) + right[...]) * scale[...]
    sums = image(trace_now, hits, spread_hits, schur, sides)
    sums_ref[...] = sums
    sent_ref[...] = sums.astype(HALF)
    deal(sums, border, first_ref, second_ref)


def last_kernel(counts, border, sides, *refs):
    parts, rest = split(counts, refs)
    right, scale, hits, couple, local, trace_ref, vol_ref = rest
    trace_now = (whole(parts, border) + right[...]) * scale[...]
    own_faces = trace_ref.shape[0]
    place = lax.axis_index("face") * own_faces
    rows = trace_now.shape[0]
    trace_ref[...] = pltpu.roll(trace_now, back(place, rows), 0)[:own_faces]
    elems = couple.shape[0]
    picked = contract(hits[...], trace_now.astype(HALF), 1, 0)
    lam = to_lanes(picked, 2 * elems, sides)
    value = local[...]
    for e in range(elems):
        value = value - contract(masked(lam, e), couple[e], 1, 1)
    vol_ref[...] = value[:elems]


def split(counts, refs):
    parts = []
    for count in counts:
        parts.append(refs[:count])
        refs = refs[count:]
    return parts, refs


def local(
    vol_inverse,
    vol_from_trace,
    trace_from_vol,
    vol_residual,
    face_ids,
    trace_residual,
    stabilization,
):
    groups = lax.axis_size("elem")
    members = lax.axis_size("face")
    chips = members // CORES
    elems, sides = face_ids.shape
    volume = vol_residual.shape[1]
    own_faces, width = trace_residual.shape
    group_faces = own_faces * members
    border = elems * members
    rows = group_faces + border
    slots = 2 * elems * sides
    trace = sides * width
    dims = (groups, elems, sides, width, group_faces, border)

    def swap_core(block):
        return lax.ppermute(block, AXES, other_core(groups, chips))

    def exchange(part, sent, to_first, to_second):
        straight = [
            [shift + core for core in range(CORES)] for shift in range(0, chips, CORES)
        ]
        second = [lax.ppermute(to_second, AXES, partners(groups, chips, 1, s)) for s in straight]
        first = [lax.ppermute(to_first, AXES, partners(groups, chips, 0, s)) for s in straight]
        own = [part] + [
            lax.ppermute(sent, AXES, along_x(groups, chips, shift)) for shift in range(1, chips)
        ]
        mate = swap_core(jnp.concatenate([block[:border] for block in (*first, *second)]))
        return own, first, second, [mate]

    down = jnp.swapaxes(trace_from_vol, 1, 2)
    large = (vol_inverse, down)
    small = (vol_residual, face_ids, trace_residual, stabilization)
    local_part, packet, ids, inverse, down = call(
        functools.partial(load_kernel, dims),
        [
            ((2 * elems, volume), F32),
            ((rows, 2 * width + sides), F32),
            ((2 * elems, sides), jnp.int32),
            *((array.shape, array.dtype) for array in large),
        ],
        *large, *small,
        stay=6,
        scratch=[
            *(pltpu.VMEM(array.shape, array.dtype) for array in small),
            pltpu.SemaphoreType.DMA((6,)),
        ],
    )
    mate = swap_core(packet)
    couple = jnp.einsum(
        "evk,ekt->evt", inverse, vol_from_trace, preferred_element_type=F32
    ).astype(HALF)
    couple, mate = lax.optimization_barrier((couple, mate))
    chip_faces = CORES * own_faces
    sums, to_first, to_second = call(
        functools.partial(join_kernel, border, width),
        [
            ((rows, 2 * width), F32),
            ((border + 16, 2 * width), F32),
            ((border, 2 * width), F32),
        ],
        packet, mate,
    )
    couple, sums = lax.optimization_barrier((couple, sums))
    schur_own = jnp.einsum("evs,evt->est", couple, down, preferred_element_type=F32).astype(HALF)
    schur_mate = swap_core(schur_own)
    hits, spread_hits = call(
        functools.partial(hits_kernel, dims),
        [((slots, rows), HALF), ((rows, slots), HALF)],
        ids, mate,
        cost=pl.CostEstimate(flops=70000000000, bytes_accessed=0, transcendentals=0),
    )

    def counted(kernel, parts):
        return functools.partial(kernel, tuple(len(part) for part in parts), border, sides)

    def flat(parts):
        return [ref for part in parts for ref in part]

    dealt = [
        ((rows, width), F32),
        ((rows, width), HALF),
        ((border, width), HALF),
        ((2 * border, width), HALF),
    ]
    sums, schur_own = lax.optimization_barrier((sums, schur_own))
    (sent,) = call(
        functools.partial(pack_kernel, chip_faces), [((rows, width + width // 2), F32)], sums
    )
    (_, *across), *rest = exchange(sums, sent, to_first, to_second)
    own = call(
        functools.partial(own_kernel, chip_faces), [((rows, 2 * width), F32)], sums, *across
    )
    parts = own, *rest
    right, scale, *out = call(
        counted(first_kernel, parts),
        [((rows, width), F32)] * 2 + dealt,
        *flat(parts), hits, spread_hits, schur_own, schur_mate,
    )
    for _ in range(SWEEPS - 2):
        parts = exchange(*out)
        out = call(
            counted(step_kernel, parts), dealt,
            *flat(parts), right, scale, hits, spread_hits, schur_own, schur_mate,
        )
    parts = exchange(*out)
    trace_update, vol_update = call(
        counted(last_kernel, parts),
        [((own_faces, width), F32), ((elems, volume), F32)],
        *flat(parts), right, scale, hits, couple, local_part,
    )
    return trace_update, vol_update


def solution(mesh):
    in_specs = (
        P(AXES, None, None),
        P(AXES, None, None),
        P(AXES, None, None),
        P(AXES, None),
        P(AXES, None),
        P(AXES, None),
        P(AXES, None),
    )
    out_specs = (P(AXES, None), P(AXES, None))
    return jax.shard_map(local, mesh=mesh, in_specs=in_specs, out_specs=out_specs, check_vma=False)
```

```python
import functools

import jax
import jax.numpy as jnp
from jax import lax
from jax.experimental import pallas as pl
from jax.experimental.pallas import tpu as pltpu
from jax.sharding import PartitionSpec as P

SWEEPS = 5
WAIT = pl.CostEstimate(flops=70 * 10**9, bytes_accessed=0, transcendentals=0)
AXES = ("elem", "face")
CORES = 2
F32 = jnp.float32
HALF = jnp.bfloat16
VMEM = pl.BlockSpec(memory_space=pltpu.VMEM)
HBM = pl.BlockSpec(memory_space=pltpu.HBM)


def partners(groups, chips, offset, shifts):
    route = []
    for group in range(groups):
        side = 1 if (group - offset) % 2 == 0 else -1
        other = (group + side) % groups
        for chip in range(chips):
            for core in range(CORES):
                target = (chip + side * shifts[core]) % chips
                route.append(
                    (
                        (group * chips + chip) * CORES + core,
                        (other * chips + target) * CORES + core,
                    )
                )
    return route


def along_x(groups, chips, shift):
    return [
        (
            (group * chips + chip) * CORES + core,
            (group * chips + (chip + shift) % chips) * CORES + (core + 1) % CORES,
        )
        for group in range(groups)
        for chip in range(chips)
        for core in range(CORES)
    ]


def other_core(groups, chips):
    return [
        (chip * CORES + core, chip * CORES + 1 - core)
        for chip in range(groups * chips)
        for core in range(CORES)
    ]


def call(body, shapes, *args, limit=16, stay=0, scratch=(), cost=None):
    outs = [jax.ShapeDtypeStruct(shape, kind) for shape, kind in shapes]
    args = [
        pltpu.with_memory_space_constraint(arg, pltpu.HBM) if n < stay else arg
        for n, arg in enumerate(args)
    ]
    return pl.pallas_call(
        body,
        out_shape=outs,
        in_specs=[HBM] * stay + [VMEM] * (len(args) - stay),
        out_specs=[VMEM] * len(outs),
        scratch_shapes=list(scratch),
        cost_estimate=cost,
        compiler_params=pltpu.CompilerParams(vmem_limit_bytes=limit * 2**20),
    )(*args)


def contract(left, right, left_dim, right_dim):
    return lax.dot_general(
        left, right, (((left_dim,), (right_dim,)), ((), ())), preferred_element_type=F32
    )


def add_up(refs):
    value = refs[0][...].astype(F32)
    for ref in refs[1:]:
        value = value + ref[...].astype(F32)
    return value


def to_lanes(rows, elems, sides):
    return jnp.concatenate([rows[elems * k : elems * (k + 1)] for k in range(sides)], axis=1)


def to_rows(lanes, sides, width):
    return jnp.concatenate([lanes[:, width * k : width * (k + 1)] for k in range(sides)], axis=0)


def spread(spread_hits, values):
    high = values.astype(HALF)
    low = (values - high.astype(F32)).astype(HALF)
    return contract(spread_hits, high, 1, 0) + contract(spread_hits, low, 1, 0)


def hit_rows(ids, rows, group_faces, border, groups):
    group = lax.axis_index("elem")
    own = ids - group * group_faces
    low = ids - lax.rem(group + groups - 1, groups) * group_faces
    place = jnp.where((own >= 0) & (own < group_faces), own, low + group_faces)
    place = jnp.where(ids < 0, -1, place)
    elems, sides = ids.shape
    lane = lax.broadcasted_iota(jnp.int32, (elems, rows), 1)
    return jnp.concatenate(
        [(place[:, k : k + 1] == lane).astype(F32) for k in range(sides)], axis=0
    )


def masked(rows, element):
    index = lax.broadcasted_iota(jnp.int32, rows.shape, 0)
    return jnp.where(index == element, rows, 0.0).astype(HALF)


def load_kernel(dims, *refs):
    groups, elems, sides, width, group_faces, border = dims
    sources, (local_ref, packet_ref, ids_ref, inverse, down, up) = refs[:7], refs[7:13]
    residual, ids, residual_rows, stab_rows, sems = refs[13:]
    rows = group_faces + border
    lines = 2 * elems

    def fetch(index, target, at, count, sem):
        piece = pl.ds(at, count)
        copy = pltpu.make_async_copy(sources[index].at[piece], target.at[piece], sems.at[sem])
        copy.start()
        return copy

    inverse_hbm, down_hbm, up_hbm, residual_hbm, ids_hbm, residual_rows_hbm, stab_rows_hbm = range(7)
    own_faces = residual_rows.shape[0]
    first = [fetch(residual_hbm, residual, 0, elems, 0), fetch(inverse_hbm, inverse, 0, elems, 1)]
    down_copy = fetch(down_hbm, down, 0, elems, 2)
    small = [
        fetch(ids_hbm, ids, 0, elems, 3),
        fetch(residual_rows_hbm, residual_rows, 0, own_faces, 4),
        fetch(stab_rows_hbm, stab_rows, 0, own_faces, 5),
    ]
    up_copy = fetch(up_hbm, up, 0, elems, 6)
    for copy in first:
        copy.wait()
    source = residual[...].astype(F32)
    source = jnp.concatenate([source, jnp.zeros_like(source)], axis=0)
    local = add_up([contract(masked(source, e), inverse[e], 1, 1) for e in range(elems)])
    local_ref[...] = local
    for copy in small:
        copy.wait()
    ids_ref[...] = jnp.full((lines, sides), -1, jnp.int32)
    ids_ref[:elems] = ids[...]
    hits = hit_rows(ids_ref[...], rows, group_faces, border, groups)
    spread_hits = hits.T.astype(HALF)
    place = lax.axis_index("face") * own_faces
    blank = jnp.zeros((rows - own_faces, width), F32)
    right = pltpu.roll(jnp.concatenate([residual_rows[...], blank], axis=0), place, 0)
    scale = pltpu.roll(jnp.concatenate([stab_rows[...], blank], axis=0), place, 0)
    packet_ref[:lines, 2 * width :] = ids_ref[...].astype(F32)
    down_copy.wait()
    load = [contract(masked(local, e), down[e], 1, 0) for e in range(elems)]
    sums = spread(spread_hits, to_rows(add_up(load), sides, width))
    packet_ref[:, : 2 * width] = jnp.concatenate([right - sums, scale], axis=1)
    up_copy.wait()


def join_kernel(border, width, packet, mate, sums_ref, first_ref, second_ref):
    sums = packet[:, : 2 * width] + mate[:, : 2 * width]
    sums_ref[...] = sums
    deal(sums, border, first_ref, second_ref)


def pack_kernel(chip_faces, sums, sent_ref):
    width = sums.shape[1] // 2
    half = width // 2
    chip = lax.axis_index("face") // CORES
    scale = pltpu.roll(sums[:, width:], back(chip * chip_faces, sums.shape[0]), 0)[:chip_faces]
    sent_ref[...] = jnp.zeros(sent_ref.shape, F32)
    sent_ref[:, :width] = sums[:, :width]
    sent_ref[:chip_faces, width:] = scale[:, :half]
    sent_ref[chip_faces : 2 * chip_faces, width:] = scale[:, half:]


def back(shift, rows):
    return lax.rem(rows - shift, rows)


def deal(sums, border, first_ref, second_ref):
    even = lax.rem(lax.axis_index("elem"), 2) == 0
    upper, lower = sums[:border], sums[sums.shape[0] - border :]
    kind = first_ref.dtype
    first_ref[:border] = jnp.where(even, upper, lower).astype(kind)
    if first_ref.shape[0] > border:
        first_ref[border:] = sums[: first_ref.shape[0] - border].astype(kind)
    second_ref[:border] = jnp.where(even, lower, upper).astype(kind)
    if second_ref.shape[0] > border:
        second_ref[border:] = sums[: second_ref.shape[0] - border].astype(kind)


def hits_kernel(dims, ids, mate, hits_ref, spread_ref):
    groups, elems, sides, width, group_faces, border = dims
    far = mate[:elems, 2 * width :].astype(jnp.int32)
    both = jnp.concatenate([ids[:elems], far], axis=0)
    hits = hit_rows(both, group_faces + border, group_faces, border, groups)
    hits_ref[...] = hits.astype(HALF)
    spread_ref[...] = hits.T.astype(HALF)


def whole(parts, border):
    own, first, second, (mate,) = parts
    even = lax.rem(lax.axis_index("elem"), 2) == 0
    blocks = mate[...].astype(F32)
    a, b = add_up(first)[:border], add_up(second)[:border]
    for n in range(len(first)):
        a = a + blocks[n * border : (n + 1) * border]
        b = b + blocks[(len(first) + n) * border : (len(first) + n + 1) * border]
    upper, lower = jnp.where(even, a, b), jnp.where(even, b, a)
    sums = add_up(own)
    last = sums.shape[0] - border
    return jnp.concatenate([sums[:border] + upper, sums[border:last], sums[last:] + lower], axis=0)


def image(trace_now, hits, spread_hits, schur, sides):
    pieces = [block[e] for block in schur for e in range(block.shape[0])]
    picked = contract(hits[...], trace_now.astype(HALF), 1, 0)
    lam = to_lanes(picked, len(pieces), sides)
    terms = add_up([contract(masked(lam, e), block, 1, 0) for e, block in enumerate(pieces)])
    return spread(spread_hits[...], to_rows(terms, sides, trace_now.shape[1]))


def own_kernel(chip_faces, sums, *refs):
    *across, total_ref = refs
    rows, width = sums.shape[0], sums.shape[1] // 2
    chip = lax.axis_index("face") // CORES
    chips = len(across) + 1
    total = sums[...]
    for n, block in enumerate(across):
        packed = block[...]
        pair = [packed[chip_faces * k : chip_faces * (k + 1), width:] for k in range(2)]
        scale = jnp.concatenate(pair, axis=1)
        scale = jnp.concatenate([scale, jnp.zeros((rows - chip_faces, width), F32)], axis=0)
        scale = pltpu.roll(scale, lax.rem(chip + chips - n - 1, chips) * chip_faces, 0)
        total = total + jnp.concatenate([packed[:, :width], scale], axis=1)
    total_ref[...] = total


def first_kernel(counts, border, sides, *refs):
    parts, rest = split(counts, refs)
    hits, spread_hits, *schur, right_ref, scale_ref, sums_ref, sent_ref, first_ref, second_ref = rest
    both = whole(parts, border)
    width = both.shape[1] // 2
    right = both[:, :width]
    scale = 1.0 / both[:, width:]
    right_ref[...] = right
    scale_ref[...] = scale
    sums = image(right * scale, hits, spread_hits, schur, sides)
    sums_ref[...] = sums
    sent_ref[...] = sums.astype(HALF)
    deal(sums, border, first_ref, second_ref)


def step_kernel(counts, border, sides, *refs):
    parts, rest = split(counts, refs)
    right, scale, hits, spread_hits, *schur, sums_ref, sent_ref, first_ref, second_ref = rest
    trace_now = (whole(parts, border) + right[...]) * scale[...]
    sums = image(trace_now, hits, spread_hits, schur, sides)
    sums_ref[...] = sums
    sent_ref[...] = sums.astype(HALF)
    deal(sums, border, first_ref, second_ref)


def last_kernel(counts, border, sides, *refs):
    parts, rest = split(counts, refs)
    right, scale, hits, couple, local, trace_ref, vol_ref = rest
    trace_now = (whole(parts, border) + right[...]) * scale[...]
    own_faces = trace_ref.shape[0]
    place = lax.axis_index("face") * own_faces
    rows = trace_now.shape[0]
    trace_ref[...] = pltpu.roll(trace_now, back(place, rows), 0)[:own_faces]
    elems = couple.shape[0]
    picked = contract(hits[...], trace_now.astype(HALF), 1, 0)
    lam = to_lanes(picked, 2 * elems, sides)
    value = local[...]
    for e in range(elems):
        value = value - contract(masked(lam, e), couple[e], 1, 1)
    vol_ref[...] = value[:elems]


def split(counts, refs):
    parts = []
    for count in counts:
        parts.append(refs[:count])
        refs = refs[count:]
    return parts, refs


def local(
    vol_inverse,
    vol_from_trace,
    trace_from_vol,
    vol_residual,
    face_ids,
    trace_residual,
    stabilization,
):
    groups = lax.axis_size("elem")
    members = lax.axis_size("face")
    chips = members // CORES
    elems, sides = face_ids.shape
    volume = vol_residual.shape[1]
    own_faces, width = trace_residual.shape
    group_faces = own_faces * members
    border = elems * members
    rows = group_faces + border
    slots = 2 * elems * sides
    trace = sides * width
    dims = (groups, elems, sides, width, group_faces, border)

    def swap_core(block):
        return lax.ppermute(block, AXES, other_core(groups, chips))

    def exchange(part, sent, to_first, to_second):
        straight = [
            [shift + core for core in range(CORES)] for shift in range(0, chips, CORES)
        ]
        second = [lax.ppermute(to_second, AXES, partners(groups, chips, 1, s)) for s in straight]
        first = [lax.ppermute(to_first, AXES, partners(groups, chips, 0, s)) for s in straight]
        own = [part] + [
            lax.ppermute(sent, AXES, along_x(groups, chips, shift)) for shift in range(1, chips)
        ]
        mate = swap_core(jnp.concatenate([block[:border] for block in (*first, *second)]))
        return own, first, second, [mate]

    down = jnp.swapaxes(trace_from_vol, 1, 2)
    large = (vol_inverse, down, vol_from_trace)
    small = (vol_residual, face_ids, trace_residual, stabilization)
    local_part, packet, ids, inverse, down, up = call(
        functools.partial(load_kernel, dims),
        [
            ((2 * elems, volume), F32),
            ((rows, 2 * width + sides), F32),
            ((2 * elems, sides), jnp.int32),
            *((array.shape, array.dtype) for array in large),
        ],
        *large, *small,
        stay=7,
        scratch=[
            *(pltpu.VMEM(array.shape, array.dtype) for array in small),
            pltpu.SemaphoreType.DMA((7,)),
        ],
    )
    mate = swap_core(packet)
    couple = jnp.einsum(
        "evk,ekt->evt", inverse, up, preferred_element_type=F32
    ).astype(HALF)
    couple, mate = lax.optimization_barrier((couple, mate))
    chip_faces = CORES * own_faces
    sums, to_first, to_second = call(
        functools.partial(join_kernel, border, width),
        [
            ((rows, 2 * width), F32),
            ((border + 16, 2 * width), F32),
            ((border, 2 * width), F32),
        ],
        packet, mate,
    )
    couple, sums = lax.optimization_barrier((couple, sums))
    schur_own = jnp.einsum("evs,evt->est", couple, down, preferred_element_type=F32).astype(HALF)
    schur_mate = swap_core(schur_own)
    hits, spread_hits = call(
        functools.partial(hits_kernel, dims),
        [((slots, rows), HALF), ((rows, slots), HALF)],
        ids, mate,
        cost=WAIT,
    )

    def counted(kernel, parts):
        return functools.partial(kernel, tuple(len(part) for part in parts), border, sides)

    def flat(parts):
        return [ref for part in parts for ref in part]

    dealt = [
        ((rows, width), F32),
        ((rows, width), HALF),
        ((border, width), HALF),
        ((2 * border, width), HALF),
    ]
    sums, schur_own = lax.optimization_barrier((sums, schur_own))
    (sent,) = call(
        functools.partial(pack_kernel, chip_faces), [((rows, width + width // 2), F32)], sums
    )
    (_, *across), *rest = exchange(sums, sent, to_first, to_second)
    own = call(
        functools.partial(own_kernel, chip_faces), [((rows, 2 * width), F32)], sums, *across
    )
    parts = own, *rest
    right, scale, *out = call(
        counted(first_kernel, parts),
        [((rows, width), F32)] * 2 + dealt,
        *flat(parts), hits, spread_hits, schur_own, schur_mate,
    )
    for _ in range(SWEEPS - 2):
        parts = exchange(*out)
        out = call(
            counted(step_kernel, parts), dealt,
            *flat(parts), right, scale, hits, spread_hits, schur_own, schur_mate,
        )
    parts = exchange(*out)
    trace_update, vol_update = call(
        counted(last_kernel, parts),
        [((own_faces, width), F32), ((elems, volume), F32)],
        *flat(parts), right, scale, hits, couple, local_part,
    )
    return trace_update, vol_update


def solution(mesh):
    in_specs = (
        P(AXES, None, None),
        P(AXES, None, None),
        P(AXES, None, None),
        P(AXES, None),
        P(AXES, None),
        P(AXES, None),
        P(AXES, None),
    )
    out_specs = (P(AXES, None), P(AXES, None))
    return jax.shard_map(local, mesh=mesh, in_specs=in_specs, out_specs=out_specs, check_vma=False)
```

```python
import functools

import jax
import jax.numpy as jnp
from jax import lax
from jax.experimental import pallas as pl
from jax.experimental.pallas import tpu as pltpu
from jax.sharding import PartitionSpec as P

SWEEPS = 5
WAIT = pl.CostEstimate(flops=70 * 10**9, bytes_accessed=0, transcendentals=0)
AXES = ("elem", "face")
CORES = 2
F32 = jnp.float32
HALF = jnp.bfloat16
VMEM = pl.BlockSpec(memory_space=pltpu.VMEM)
HBM = pl.BlockSpec(memory_space=pltpu.HBM)


def partners(groups, chips, offset, shifts):
    route = []
    for group in range(groups):
        side = 1 if (group - offset) % 2 == 0 else -1
        other = (group + side) % groups
        for chip in range(chips):
            for core in range(CORES):
                target = (chip + side * shifts[core]) % chips
                route.append(
                    (
                        (group * chips + chip) * CORES + core,
                        (other * chips + target) * CORES + core,
                    )
                )
    return route


def along_x(groups, chips, shift):
    return [
        (
            (group * chips + chip) * CORES + core,
            (group * chips + (chip + shift) % chips) * CORES + (core + 1) % CORES,
        )
        for group in range(groups)
        for chip in range(chips)
        for core in range(CORES)
    ]


def other_core(groups, chips):
    return [
        (chip * CORES + core, chip * CORES + 1 - core)
        for chip in range(groups * chips)
        for core in range(CORES)
    ]


def call(body, shapes, *args, limit=16, stay=0, scratch=(), cost=None):
    outs = [jax.ShapeDtypeStruct(shape, kind) for shape, kind in shapes]
    args = [
        pltpu.with_memory_space_constraint(arg, pltpu.HBM) if n < stay else arg
        for n, arg in enumerate(args)
    ]
    return pl.pallas_call(
        body,
        out_shape=outs,
        in_specs=[HBM] * stay + [VMEM] * (len(args) - stay),
        out_specs=[VMEM] * len(outs),
        scratch_shapes=list(scratch),
        cost_estimate=cost,
        compiler_params=pltpu.CompilerParams(vmem_limit_bytes=limit * 2**20),
    )(*args)


def contract(left, right, left_dim, right_dim):
    return lax.dot_general(
        left, right, (((left_dim,), (right_dim,)), ((), ())), preferred_element_type=F32
    )


def add_up(refs):
    value = refs[0][...].astype(F32)
    for ref in refs[1:]:
        value = value + ref[...].astype(F32)
    return value


def to_lanes(rows, elems, sides):
    return jnp.concatenate([rows[elems * k : elems * (k + 1)] for k in range(sides)], axis=1)


def to_rows(lanes, sides, width):
    return jnp.concatenate([lanes[:, width * k : width * (k + 1)] for k in range(sides)], axis=0)


def spread(spread_hits, values):
    high = values.astype(HALF)
    low = (values - high.astype(F32)).astype(HALF)
    return contract(spread_hits, high, 1, 0) + contract(spread_hits, low, 1, 0)


def hit_rows(ids, rows, group_faces, border, groups):
    group = lax.axis_index("elem")
    own = ids - group * group_faces
    low = ids - lax.rem(group + groups - 1, groups) * group_faces
    place = jnp.where((own >= 0) & (own < group_faces), own, low + group_faces)
    place = jnp.where(ids < 0, -1, place)
    elems, sides = ids.shape
    lane = lax.broadcasted_iota(jnp.int32, (elems, rows), 1)
    return jnp.concatenate(
        [(place[:, k : k + 1] == lane).astype(F32) for k in range(sides)], axis=0
    )


def masked(rows, element):
    index = lax.broadcasted_iota(jnp.int32, rows.shape, 0)
    return jnp.where(index == element, rows, 0.0).astype(HALF)


def load_kernel(dims, *refs):
    groups, elems, sides, width, group_faces, border = dims
    sources, (local_ref, packet_ref, ids_ref, inverse, down, up) = refs[:7], refs[7:13]
    residual, ids, residual_rows, stab_rows, sems = refs[13:]
    rows = group_faces + border
    lines = 2 * elems

    def fetch(index, target, at, count, sem):
        piece = pl.ds(at, count)
        copy = pltpu.make_async_copy(sources[index].at[piece], target.at[piece], sems.at[sem])
        copy.start()
        return copy

    inverse_hbm, down_hbm, up_hbm, residual_hbm, ids_hbm, residual_rows_hbm, stab_rows_hbm = range(7)
    own_faces = residual_rows.shape[0]
    first = [fetch(residual_hbm, residual, 0, elems, 0), fetch(inverse_hbm, inverse, 0, elems, 1)]
    down_copy = fetch(down_hbm, down, 0, elems, 2)
    small = [
        fetch(ids_hbm, ids, 0, elems, 3),
        fetch(residual_rows_hbm, residual_rows, 0, own_faces, 4),
        fetch(stab_rows_hbm, stab_rows, 0, own_faces, 5),
    ]
    up_copy = fetch(up_hbm, up, 0, elems, 6)
    for copy in first:
        copy.wait()
    source = residual[...].astype(F32)
    source = jnp.concatenate([source, jnp.zeros_like(source)], axis=0)
    local = add_up([contract(masked(source, e), inverse[e], 1, 1) for e in range(elems)])
    local_ref[...] = local
    for copy in small:
        copy.wait()
    ids_ref[...] = jnp.full((lines, sides), -1, jnp.int32)
    ids_ref[:elems] = ids[...]
    hits = hit_rows(ids_ref[...], rows, group_faces, border, groups)
    spread_hits = hits.T.astype(HALF)
    place = lax.axis_index("face") * own_faces
    blank = jnp.zeros((rows - own_faces, width), F32)
    right = pltpu.roll(jnp.concatenate([residual_rows[...], blank], axis=0), place, 0)
    scale = pltpu.roll(jnp.concatenate([stab_rows[...], blank], axis=0), place, 0)
    packet_ref[:lines, 2 * width :] = ids_ref[...].astype(F32)
    down_copy.wait()
    load = [contract(masked(local, e), down[e], 1, 0) for e in range(elems)]
    sums = spread(spread_hits, to_rows(add_up(load), sides, width))
    packet_ref[:, : 2 * width] = jnp.concatenate([right - sums, scale], axis=1)
    up_copy.wait()


def join_kernel(border, width, packet, mate, sums_ref, first_ref, second_ref):
    sums = packet[:, : 2 * width] + mate[:, : 2 * width]
    sums_ref[...] = sums
    deal(sums, border, first_ref, second_ref)


def pack_kernel(chip_faces, sums, sent_ref):
    width = sums.shape[1] // 2
    half = width // 2
    chip = lax.axis_index("face") // CORES
    scale = pltpu.roll(sums[:, width:], back(chip * chip_faces, sums.shape[0]), 0)[:chip_faces]
    sent_ref[...] = jnp.zeros(sent_ref.shape, F32)
    sent_ref[:, :width] = sums[:, :width]
    sent_ref[:chip_faces, width:] = scale[:, :half]
    sent_ref[chip_faces : 2 * chip_faces, width:] = scale[:, half:]


def back(shift, rows):
    return lax.rem(rows - shift, rows)


def deal(sums, border, first_ref, second_ref):
    even = lax.rem(lax.axis_index("elem"), 2) == 0
    upper, lower = sums[:border], sums[sums.shape[0] - border :]
    kind = first_ref.dtype
    first_ref[:border] = jnp.where(even, upper, lower).astype(kind)
    if first_ref.shape[0] > border:
        first_ref[border:] = sums[: first_ref.shape[0] - border].astype(kind)
    second_ref[:border] = jnp.where(even, lower, upper).astype(kind)
    if second_ref.shape[0] > border:
        second_ref[border:] = sums[: second_ref.shape[0] - border].astype(kind)


def hits_kernel(dims, ids, mate, hits_ref, spread_ref):
    groups, elems, sides, width, group_faces, border = dims
    far = mate[:elems, 2 * width :].astype(jnp.int32)
    both = jnp.concatenate([ids[:elems], far], axis=0)
    hits = hit_rows(both, group_faces + border, group_faces, border, groups)
    hits_ref[...] = hits.astype(HALF)
    spread_ref[...] = hits.T.astype(HALF)


def whole(parts, border):
    own, first, second, (mate,) = parts
    even = lax.rem(lax.axis_index("elem"), 2) == 0
    blocks = mate[...].astype(F32)
    a, b = add_up(first)[:border], add_up(second)[:border]
    for n in range(len(first)):
        a = a + blocks[n * border : (n + 1) * border]
        b = b + blocks[(len(first) + n) * border : (len(first) + n + 1) * border]
    upper, lower = jnp.where(even, a, b), jnp.where(even, b, a)
    sums = add_up(own)
    last = sums.shape[0] - border
    return jnp.concatenate([sums[:border] + upper, sums[border:last], sums[last:] + lower], axis=0)


def image(trace_now, hits, spread_hits, schur, sides):
    pieces = [block[e] for block in schur for e in range(block.shape[0])]
    picked = contract(hits[...], trace_now.astype(HALF), 1, 0)
    lam = to_lanes(picked, len(pieces), sides)
    terms = add_up([contract(masked(lam, e), block, 1, 0) for e, block in enumerate(pieces)])
    return spread(spread_hits[...], to_rows(terms, sides, trace_now.shape[1]))


def own_kernel(chip_faces, sums, *refs):
    *across, total_ref = refs
    rows, width = sums.shape[0], sums.shape[1] // 2
    chip = lax.axis_index("face") // CORES
    chips = len(across) + 1
    total = sums[...]
    for n, block in enumerate(across):
        packed = block[...]
        pair = [packed[chip_faces * k : chip_faces * (k + 1), width:] for k in range(2)]
        scale = jnp.concatenate(pair, axis=1)
        scale = jnp.concatenate([scale, jnp.zeros((rows - chip_faces, width), F32)], axis=0)
        scale = pltpu.roll(scale, lax.rem(chip + chips - n - 1, chips) * chip_faces, 0)
        total = total + jnp.concatenate([packed[:, :width], scale], axis=1)
    total_ref[...] = total


def first_kernel(counts, border, sides, *refs):
    parts, rest = split(counts, refs)
    hits, spread_hits, *schur, right_ref, scale_ref, sums_ref, sent_ref, first_ref, second_ref = rest
    both = whole(parts, border)
    width = both.shape[1] // 2
    right = both[:, :width]
    scale = 1.0 / both[:, width:]
    right_ref[...] = right
    scale_ref[...] = scale
    sums = image(right * scale, hits, spread_hits, schur, sides)
    sums_ref[...] = sums
    sent_ref[...] = sums.astype(HALF)
    deal(sums, border, first_ref, second_ref)


def step_kernel(counts, border, sides, *refs):
    parts, rest = split(counts, refs)
    right, scale, hits, spread_hits, *schur, sums_ref, sent_ref, first_ref, second_ref = rest
    trace_now = (whole(parts, border) + right[...]) * scale[...]
    sums = image(trace_now, hits, spread_hits, schur, sides)
    sums_ref[...] = sums
    sent_ref[...] = sums.astype(HALF)
    deal(sums, border, first_ref, second_ref)


def turn_kernel(couple, after, turned_ref):
    for e in range(couple.shape[0]):
        turned_ref[e] = couple[e].T


def last_kernel(counts, border, sides, *refs):
    parts, rest = split(counts, refs)
    right, scale, hits, couple, local, trace_ref, vol_ref = rest
    trace_now = (whole(parts, border) + right[...]) * scale[...]
    own_faces = trace_ref.shape[0]
    place = lax.axis_index("face") * own_faces
    rows = trace_now.shape[0]
    trace_ref[...] = pltpu.roll(trace_now, back(place, rows), 0)[:own_faces]
    elems = couple.shape[0]
    picked = contract(hits[...], trace_now.astype(HALF), 1, 0)
    lam = to_lanes(picked, 2 * elems, sides)
    value = local[...]
    for e in range(elems):
        value = value - contract(masked(lam, e), couple[e], 1, 0)
    vol_ref[...] = value[:elems]


def split(counts, refs):
    parts = []
    for count in counts:
        parts.append(refs[:count])
        refs = refs[count:]
    return parts, refs


def local(
    vol_inverse,
    vol_from_trace,
    trace_from_vol,
    vol_residual,
    face_ids,
    trace_residual,
    stabilization,
):
    groups = lax.axis_size("elem")
    members = lax.axis_size("face")
    chips = members // CORES
    elems, sides = face_ids.shape
    volume = vol_residual.shape[1]
    own_faces, width = trace_residual.shape
    group_faces = own_faces * members
    border = elems * members
    rows = group_faces + border
    slots = 2 * elems * sides
    trace = sides * width
    dims = (groups, elems, sides, width, group_faces, border)

    def swap_core(block):
        return lax.ppermute(block, AXES, other_core(groups, chips))

    def exchange(part, sent, to_first, to_second):
        straight = [
            [shift + core for core in range(CORES)] for shift in range(0, chips, CORES)
        ]
        second = [lax.ppermute(to_second, AXES, partners(groups, chips, 1, s)) for s in straight]
        first = [lax.ppermute(to_first, AXES, partners(groups, chips, 0, s)) for s in straight]
        own = [part] + [
            lax.ppermute(sent, AXES, along_x(groups, chips, shift)) for shift in range(1, chips)
        ]
        mate = swap_core(jnp.concatenate([block[:border] for block in (*first, *second)]))
        return own, first, second, [mate]

    down = jnp.swapaxes(trace_from_vol, 1, 2)
    large = (vol_inverse, down, vol_from_trace)
    small = (vol_residual, face_ids, trace_residual, stabilization)
    local_part, packet, ids, inverse, down, up = call(
        functools.partial(load_kernel, dims),
        [
            ((2 * elems, volume), F32),
            ((rows, 2 * width + sides), F32),
            ((2 * elems, sides), jnp.int32),
            *((array.shape, array.dtype) for array in large),
        ],
        *large, *small,
        stay=7,
        scratch=[
            *(pltpu.VMEM(array.shape, array.dtype) for array in small),
            pltpu.SemaphoreType.DMA((7,)),
        ],
    )
    mate = swap_core(packet)
    couple = jnp.einsum(
        "evk,ekt->evt", inverse, up, preferred_element_type=F32
    ).astype(HALF)
    couple, mate = lax.optimization_barrier((couple, mate))
    chip_faces = CORES * own_faces
    sums, to_first, to_second = call(
        functools.partial(join_kernel, border, width),
        [
            ((rows, 2 * width), F32),
            ((border + 16, 2 * width), F32),
            ((border, 2 * width), F32),
        ],
        packet, mate,
    )
    couple, sums = lax.optimization_barrier((couple, sums))
    schur_own = jnp.einsum("evs,evt->est", couple, down, preferred_element_type=F32).astype(HALF)
    schur_mate = swap_core(schur_own)
    hits, spread_hits = call(
        functools.partial(hits_kernel, dims),
        [((slots, rows), HALF), ((rows, slots), HALF)],
        ids, mate,
        cost=WAIT,
    )

    def counted(kernel, parts):
        return functools.partial(kernel, tuple(len(part) for part in parts), border, sides)

    def flat(parts):
        return [ref for part in parts for ref in part]

    dealt = [
        ((rows, width), F32),
        ((rows, width), HALF),
        ((border, width), HALF),
        ((2 * border, width), HALF),
    ]
    sums, schur_own = lax.optimization_barrier((sums, schur_own))
    (sent,) = call(
        functools.partial(pack_kernel, chip_faces), [((rows, width + width // 2), F32)], sums
    )
    (_, *across), *rest = exchange(sums, sent, to_first, to_second)
    own = call(
        functools.partial(own_kernel, chip_faces), [((rows, 2 * width), F32)], sums, *across
    )
    parts = own, *rest
    right, scale, *out = call(
        counted(first_kernel, parts),
        [((rows, width), F32)] * 2 + dealt,
        *flat(parts), hits, spread_hits, schur_own, schur_mate,
    )
    (turned,) = call(
        turn_kernel, [((elems, trace, volume), HALF)], couple, right,
        cost=pl.CostEstimate(flops=10**9, bytes_accessed=0, transcendentals=0),
    )
    for _ in range(SWEEPS - 2):
        parts = exchange(*out)
        out = call(
            counted(step_kernel, parts), dealt,
            *flat(parts), right, scale, hits, spread_hits, schur_own, schur_mate,
        )
    parts = exchange(*out)
    trace_update, vol_update = call(
        counted(last_kernel, parts),
        [((own_faces, width), F32), ((elems, volume), F32)],
        *flat(parts), right, scale, hits, turned, local_part,
    )
    return trace_update, vol_update


def solution(mesh):
    in_specs = (
        P(AXES, None, None),
        P(AXES, None, None),
        P(AXES, None, None),
        P(AXES, None),
        P(AXES, None),
        P(AXES, None),
        P(AXES, None),
    )
    out_specs = (P(AXES, None), P(AXES, None))
    return jax.shard_map(local, mesh=mesh, in_specs=in_specs, out_specs=out_specs, check_vma=False)
```

```python
import functools

import jax
import jax.numpy as jnp
from jax import lax
from jax.experimental import pallas as pl
from jax.experimental.pallas import tpu as pltpu
from jax.sharding import PartitionSpec as P

SWEEPS = 5
WAIT = pl.CostEstimate(flops=70 * 10**9, bytes_accessed=0, transcendentals=0)
AXES = ("elem", "face")
CORES = 2
F32 = jnp.float32
HALF = jnp.bfloat16
VMEM = pl.BlockSpec(memory_space=pltpu.VMEM)
HBM = pl.BlockSpec(memory_space=pltpu.HBM)


def partners(groups, chips, offset, shifts):
    route = []
    for group in range(groups):
        side = 1 if (group - offset) % 2 == 0 else -1
        other = (group + side) % groups
        for chip in range(chips):
            for core in range(CORES):
                target = (chip + side * shifts[core]) % chips
                route.append(
                    (
                        (group * chips + chip) * CORES + core,
                        (other * chips + target) * CORES + core,
                    )
                )
    return route


def along_x(groups, chips, shift):
    return [
        (
            (group * chips + chip) * CORES + core,
            (group * chips + (chip + shift) % chips) * CORES + (core + 1) % CORES,
        )
        for group in range(groups)
        for chip in range(chips)
        for core in range(CORES)
    ]


def other_core(groups, chips):
    return [
        (chip * CORES + core, chip * CORES + 1 - core)
        for chip in range(groups * chips)
        for core in range(CORES)
    ]


def call(body, shapes, *args, limit=16, stay=0, scratch=(), cost=None):
    outs = [jax.ShapeDtypeStruct(shape, kind) for shape, kind in shapes]
    args = [
        pltpu.with_memory_space_constraint(arg, pltpu.HBM) if n < stay else arg
        for n, arg in enumerate(args)
    ]
    return pl.pallas_call(
        body,
        out_shape=outs,
        in_specs=[HBM] * stay + [VMEM] * (len(args) - stay),
        out_specs=[VMEM] * len(outs),
        scratch_shapes=list(scratch),
        cost_estimate=cost,
        compiler_params=pltpu.CompilerParams(vmem_limit_bytes=limit * 2**20),
    )(*args)


def contract(left, right, left_dim, right_dim):
    return lax.dot_general(
        left, right, (((left_dim,), (right_dim,)), ((), ())), preferred_element_type=F32
    )


def add_up(refs):
    value = refs[0][...].astype(F32)
    for ref in refs[1:]:
        value = value + ref[...].astype(F32)
    return value


def to_lanes(rows, elems, sides):
    return jnp.concatenate([rows[elems * k : elems * (k + 1)] for k in range(sides)], axis=1)


def to_rows(lanes, sides, width):
    return jnp.concatenate([lanes[:, width * k : width * (k + 1)] for k in range(sides)], axis=0)


def spread(spread_hits, values):
    high = values.astype(HALF)
    low = (values - high.astype(F32)).astype(HALF)
    return contract(spread_hits, high, 1, 0) + contract(spread_hits, low, 1, 0)


def hit_rows(ids, rows, group_faces, border, groups):
    group = lax.axis_index("elem")
    own = ids - group * group_faces
    low = ids - lax.rem(group + groups - 1, groups) * group_faces
    place = jnp.where((own >= 0) & (own < group_faces), own, low + group_faces)
    place = jnp.where(ids < 0, -1, place)
    elems, sides = ids.shape
    lane = lax.broadcasted_iota(jnp.int32, (elems, rows), 1)
    return jnp.concatenate(
        [(place[:, k : k + 1] == lane).astype(F32) for k in range(sides)], axis=0
    )


def masked(rows, element):
    index = lax.broadcasted_iota(jnp.int32, rows.shape, 0)
    return jnp.where(index == element, rows, 0.0).astype(HALF)


def load_kernel(dims, *refs):
    groups, elems, sides, width, group_faces, border = dims
    sources, (local_ref, packet_ref, ids_ref, inverse, down, up) = refs[:7], refs[7:13]
    residual, ids, residual_rows, stab_rows, sems = refs[13:]
    rows = group_faces + border
    lines = 2 * elems

    def fetch(index, target, at, count, sem):
        piece = pl.ds(at, count)
        copy = pltpu.make_async_copy(sources[index].at[piece], target.at[piece], sems.at[sem])
        copy.start()
        return copy

    inverse_hbm, down_hbm, up_hbm, residual_hbm, ids_hbm, residual_rows_hbm, stab_rows_hbm = range(7)
    own_faces = residual_rows.shape[0]
    first = [fetch(residual_hbm, residual, 0, elems, 0), fetch(inverse_hbm, inverse, 0, elems, 1)]
    down_copy = fetch(down_hbm, down, 0, elems, 2)
    small = [
        fetch(ids_hbm, ids, 0, elems, 3),
        fetch(residual_rows_hbm, residual_rows, 0, own_faces, 4),
        fetch(stab_rows_hbm, stab_rows, 0, own_faces, 5),
    ]
    up_copy = fetch(up_hbm, up, 0, elems, 6)
    for copy in first:
        copy.wait()
    source = residual[...].astype(F32)
    source = jnp.concatenate([source, jnp.zeros_like(source)], axis=0)
    local = add_up([contract(masked(source, e), inverse[e], 1, 1) for e in range(elems)])
    local_ref[...] = local
    for copy in small:
        copy.wait()
    ids_ref[...] = jnp.full((lines, sides), -1, jnp.int32)
    ids_ref[:elems] = ids[...]
    hits = hit_rows(ids_ref[...], rows, group_faces, border, groups)
    spread_hits = hits.T.astype(HALF)
    place = lax.axis_index("face") * own_faces
    blank = jnp.zeros((rows - own_faces, width), F32)
    right = pltpu.roll(jnp.concatenate([residual_rows[...], blank], axis=0), place, 0)
    scale = pltpu.roll(jnp.concatenate([stab_rows[...], blank], axis=0), place, 0)
    packet_ref[:lines, 2 * width :] = ids_ref[...].astype(F32)
    down_copy.wait()
    load = [contract(masked(local, e), down[e], 1, 0) for e in range(elems)]
    sums = spread(spread_hits, to_rows(add_up(load), sides, width))
    packet_ref[:, : 2 * width] = jnp.concatenate([right - sums, scale], axis=1)
    up_copy.wait()


def join_kernel(border, width, packet, mate, sums_ref, first_ref, second_ref):
    sums = packet[:, : 2 * width] + mate[:, : 2 * width]
    sums_ref[...] = sums
    deal(sums, border, first_ref, second_ref)


def pack_kernel(chip_faces, sums, sent_ref):
    width = sums.shape[1] // 2
    half = width // 2
    chip = lax.axis_index("face") // CORES
    scale = pltpu.roll(sums[:, width:], back(chip * chip_faces, sums.shape[0]), 0)[:chip_faces]
    sent_ref[...] = jnp.zeros(sent_ref.shape, F32)
    sent_ref[:, :width] = sums[:, :width]
    sent_ref[:chip_faces, width:] = scale[:, :half]
    sent_ref[chip_faces : 2 * chip_faces, width:] = scale[:, half:]


def back(shift, rows):
    return lax.rem(rows - shift, rows)


def deal(sums, border, first_ref, second_ref):
    even = lax.rem(lax.axis_index("elem"), 2) == 0
    upper, lower = sums[:border], sums[sums.shape[0] - border :]
    kind = first_ref.dtype
    first_ref[:border] = jnp.where(even, upper, lower).astype(kind)
    if first_ref.shape[0] > border:
        first_ref[border:] = sums[: first_ref.shape[0] - border].astype(kind)
    second_ref[:border] = jnp.where(even, lower, upper).astype(kind)
    if second_ref.shape[0] > border:
        second_ref[border:] = sums[: second_ref.shape[0] - border].astype(kind)


def hits_kernel(dims, ids, mate, hits_ref, spread_ref):
    groups, elems, sides, width, group_faces, border = dims
    far = mate[:elems, 2 * width :].astype(jnp.int32)
    both = jnp.concatenate([ids[:elems], far], axis=0)
    hits = hit_rows(both, group_faces + border, group_faces, border, groups)
    hits_ref[...] = hits.astype(HALF)
    spread_ref[...] = hits.T.astype(HALF)


def whole(parts, border):
    own, first, second, (mate,) = parts
    even = lax.rem(lax.axis_index("elem"), 2) == 0
    blocks = mate[...].astype(F32)
    a, b = add_up(first)[:border], add_up(second)[:border]
    for n in range(len(first)):
        a = a + blocks[n * border : (n + 1) * border]
        b = b + blocks[(len(first) + n) * border : (len(first) + n + 1) * border]
    upper, lower = jnp.where(even, a, b), jnp.where(even, b, a)
    sums = add_up(own)
    last = sums.shape[0] - border
    return jnp.concatenate([sums[:border] + upper, sums[border:last], sums[last:] + lower], axis=0)


def known_kernel(counts, border, *refs):
    (own, first, second), (right, known_ref) = split(counts, refs)
    even = lax.rem(lax.axis_index("elem"), 2) == 0
    a, b = add_up(first)[:border], add_up(second)[:border]
    upper, lower = jnp.where(even, a, b), jnp.where(even, b, a)
    last = known_ref.shape[0] - border
    known_ref[...] = add_up(own) + right[...]
    known_ref[:border] += upper
    known_ref[last:] += lower


def completed(known, mate, border):
    even = lax.rem(lax.axis_index("elem"), 2) == 0
    half = mate.shape[0] // 2
    a, b = (
        add_up([mate.at[pl.ds(at + n * border, border)] for n in range(half // border)])
        for at in (0, half)
    )
    upper, lower = jnp.where(even, a, b), jnp.where(even, b, a)
    sums = known[...]
    last = sums.shape[0] - border
    return jnp.concatenate([sums[:border] + upper, sums[border:last], sums[last:] + lower], axis=0)


def image(trace_now, hits, spread_hits, schur, sides):
    pieces = [block[e] for block in schur for e in range(block.shape[0])]
    picked = contract(hits[...], trace_now.astype(HALF), 1, 0)
    lam = to_lanes(picked, len(pieces), sides)
    terms = add_up([contract(masked(lam, e), block, 1, 0) for e, block in enumerate(pieces)])
    return spread(spread_hits[...], to_rows(terms, sides, trace_now.shape[1]))


def own_kernel(chip_faces, sums, *refs):
    *across, total_ref = refs
    rows, width = sums.shape[0], sums.shape[1] // 2
    chip = lax.axis_index("face") // CORES
    chips = len(across) + 1
    total = sums[...]
    for n, block in enumerate(across):
        packed = block[...]
        pair = [packed[chip_faces * k : chip_faces * (k + 1), width:] for k in range(2)]
        scale = jnp.concatenate(pair, axis=1)
        scale = jnp.concatenate([scale, jnp.zeros((rows - chip_faces, width), F32)], axis=0)
        scale = pltpu.roll(scale, lax.rem(chip + chips - n - 1, chips) * chip_faces, 0)
        total = total + jnp.concatenate([packed[:, :width], scale], axis=1)
    total_ref[...] = total


def first_kernel(counts, border, sides, *refs):
    parts, rest = split(counts, refs)
    hits, spread_hits, *schur, right_ref, scale_ref, sums_ref, sent_ref, first_ref, second_ref = rest
    both = whole(parts, border)
    width = both.shape[1] // 2
    right = both[:, :width]
    scale = 1.0 / both[:, width:]
    right_ref[...] = right
    scale_ref[...] = scale
    sums = image(right * scale, hits, spread_hits, schur, sides)
    sums_ref[...] = sums
    sent_ref[...] = sums.astype(HALF)
    deal(sums, border, first_ref, second_ref)


def step_kernel(border, sides, known, mate, *rest):
    scale, hits, spread_hits, *schur, sums_ref, sent_ref, first_ref, second_ref = rest
    trace_now = completed(known, mate, border) * scale[...]
    sums = image(trace_now, hits, spread_hits, schur, sides)
    sums_ref[...] = sums
    sent_ref[...] = sums.astype(HALF)
    deal(sums, border, first_ref, second_ref)


def turn_kernel(couple, after, turned_ref):
    for e in range(couple.shape[0]):
        turned_ref[e] = couple[e].T


def last_kernel(border, sides, known, mate, *rest):
    scale, hits, couple, local, trace_ref, vol_ref = rest
    trace_now = completed(known, mate, border) * scale[...]
    own_faces = trace_ref.shape[0]
    place = lax.axis_index("face") * own_faces
    rows = trace_now.shape[0]
    trace_ref[...] = pltpu.roll(trace_now, back(place, rows), 0)[:own_faces]
    elems = couple.shape[0]
    picked = contract(hits[...], trace_now.astype(HALF), 1, 0)
    lam = to_lanes(picked, 2 * elems, sides)
    value = local[...]
    for e in range(elems):
        value = value - contract(masked(lam, e), couple[e], 1, 0)
    vol_ref[...] = value[:elems]


def split(counts, refs):
    parts = []
    for count in counts:
        parts.append(refs[:count])
        refs = refs[count:]
    return parts, refs


def local(
    vol_inverse,
    vol_from_trace,
    trace_from_vol,
    vol_residual,
    face_ids,
    trace_residual,
    stabilization,
):
    groups = lax.axis_size("elem")
    members = lax.axis_size("face")
    chips = members // CORES
    elems, sides = face_ids.shape
    volume = vol_residual.shape[1]
    own_faces, width = trace_residual.shape
    group_faces = own_faces * members
    border = elems * members
    rows = group_faces + border
    slots = 2 * elems * sides
    trace = sides * width
    dims = (groups, elems, sides, width, group_faces, border)

    def swap_core(block):
        return lax.ppermute(block, AXES, other_core(groups, chips))

    def exchange(part, sent, to_first, to_second):
        straight = [
            [shift + core for core in range(CORES)] for shift in range(0, chips, CORES)
        ]
        second = [lax.ppermute(to_second, AXES, partners(groups, chips, 1, s)) for s in straight]
        first = [lax.ppermute(to_first, AXES, partners(groups, chips, 0, s)) for s in straight]
        own = [part] + [
            lax.ppermute(sent, AXES, along_x(groups, chips, shift)) for shift in range(1, chips)
        ]
        mate = swap_core(jnp.concatenate([block[:border] for block in (*first, *second)]))
        return own, first, second, [mate]

    down = jnp.swapaxes(trace_from_vol, 1, 2)
    large = (vol_inverse, down, vol_from_trace)
    small = (vol_residual, face_ids, trace_residual, stabilization)
    local_part, packet, ids, inverse, down, up = call(
        functools.partial(load_kernel, dims),
        [
            ((2 * elems, volume), F32),
            ((rows, 2 * width + sides), F32),
            ((2 * elems, sides), jnp.int32),
            *((array.shape, array.dtype) for array in large),
        ],
        *large, *small,
        stay=7,
        scratch=[
            *(pltpu.VMEM(array.shape, array.dtype) for array in small),
            pltpu.SemaphoreType.DMA((7,)),
        ],
    )
    mate = swap_core(packet)
    couple = jnp.einsum(
        "evk,ekt->evt", inverse, up, preferred_element_type=F32
    ).astype(HALF)
    couple, mate = lax.optimization_barrier((couple, mate))
    chip_faces = CORES * own_faces
    sums, to_first, to_second = call(
        functools.partial(join_kernel, border, width),
        [
            ((rows, 2 * width), F32),
            ((border + 16, 2 * width), F32),
            ((border, 2 * width), F32),
        ],
        packet, mate,
    )
    couple, sums = lax.optimization_barrier((couple, sums))
    schur_own = jnp.einsum("evs,evt->est", couple, down, preferred_element_type=F32).astype(HALF)
    schur_mate = swap_core(schur_own)
    hits, spread_hits = call(
        functools.partial(hits_kernel, dims),
        [((slots, rows), HALF), ((rows, slots), HALF)],
        ids, mate,
        cost=WAIT,
    )

    def counted(kernel, parts):
        return functools.partial(kernel, tuple(len(part) for part in parts), border, sides)

    def flat(parts):
        return [ref for part in parts for ref in part]

    dealt = [
        ((rows, width), F32),
        ((rows, width), HALF),
        ((border, width), HALF),
        ((2 * border, width), HALF),
    ]
    sums, schur_own = lax.optimization_barrier((sums, schur_own))
    (sent,) = call(
        functools.partial(pack_kernel, chip_faces), [((rows, width + width // 2), F32)], sums
    )
    (_, *across), *rest = exchange(sums, sent, to_first, to_second)
    own = call(
        functools.partial(own_kernel, chip_faces), [((rows, 2 * width), F32)], sums, *across
    )
    parts = own, *rest
    right, scale, *out = call(
        counted(first_kernel, parts),
        [((rows, width), F32)] * 2 + dealt,
        *flat(parts), hits, spread_hits, schur_own, schur_mate,
    )
    (turned,) = call(
        turn_kernel, [((elems, trace, volume), HALF)], couple, right,
        cost=pl.CostEstimate(flops=10**9, bytes_accessed=0, transcendentals=0),
    )

    def gathered(*sent_parts):
        *parts, (mate,) = exchange(*sent_parts)
        counts = tuple(len(part) for part in parts)
        (known,) = call(
            functools.partial(known_kernel, counts, border), [((rows, width), F32)],
            *flat(parts), right,
        )
        return known, mate

    for _ in range(SWEEPS - 2):
        out = call(
            functools.partial(step_kernel, border, sides), dealt,
            *gathered(*out), scale, hits, spread_hits, schur_own, schur_mate,
        )
    trace_update, vol_update = call(
        functools.partial(last_kernel, border, sides),
        [((own_faces, width), F32), ((elems, volume), F32)],
        *gathered(*out), scale, hits, turned, local_part,
    )
    return trace_update, vol_update


def solution(mesh):
    in_specs = (
        P(AXES, None, None),
        P(AXES, None, None),
        P(AXES, None, None),
        P(AXES, None),
        P(AXES, None),
        P(AXES, None),
        P(AXES, None),
    )
    out_specs = (P(AXES, None), P(AXES, None))
    return jax.shard_map(local, mesh=mesh, in_specs=in_specs, out_specs=out_specs, check_vma=False)
```

```python
import functools

import jax
import jax.numpy as jnp
from jax import lax
from jax.experimental import pallas as pl
from jax.experimental.pallas import tpu as pltpu
from jax.sharding import PartitionSpec as P

SWEEPS = 5
WAIT = pl.CostEstimate(flops=70 * 10**9, bytes_accessed=0, transcendentals=0)
AXES = ("elem", "face")
CORES = 2
F32 = jnp.float32
HALF = jnp.bfloat16
VMEM = pl.BlockSpec(memory_space=pltpu.VMEM)
HBM = pl.BlockSpec(memory_space=pltpu.HBM)


def partners(groups, chips, offset, shifts):
    route = []
    for group in range(groups):
        side = 1 if (group - offset) % 2 == 0 else -1
        other = (group + side) % groups
        for chip in range(chips):
            for core in range(CORES):
                target = (chip + side * shifts[core]) % chips
                route.append(
                    (
                        (group * chips + chip) * CORES + core,
                        (other * chips + target) * CORES + core,
                    )
                )
    return route


def along_x(groups, chips, shift):
    return [
        (
            (group * chips + chip) * CORES + core,
            (group * chips + (chip + shift) % chips) * CORES + (core + 1) % CORES,
        )
        for group in range(groups)
        for chip in range(chips)
        for core in range(CORES)
    ]


def other_core(groups, chips):
    return [
        (chip * CORES + core, chip * CORES + 1 - core)
        for chip in range(groups * chips)
        for core in range(CORES)
    ]


def call(body, shapes, *args, limit=16, stay=0, scratch=(), cost=None):
    outs = [jax.ShapeDtypeStruct(shape, kind) for shape, kind in shapes]
    args = [
        pltpu.with_memory_space_constraint(arg, pltpu.HBM) if n < stay else arg
        for n, arg in enumerate(args)
    ]
    return pl.pallas_call(
        body,
        out_shape=outs,
        in_specs=[HBM] * stay + [VMEM] * (len(args) - stay),
        out_specs=[VMEM] * len(outs),
        scratch_shapes=list(scratch),
        cost_estimate=cost,
        compiler_params=pltpu.CompilerParams(vmem_limit_bytes=limit * 2**20),
    )(*args)


def contract(left, right, left_dim, right_dim):
    return lax.dot_general(
        left, right, (((left_dim,), (right_dim,)), ((), ())), preferred_element_type=F32
    )


def add_up(refs):
    value = refs[0][...].astype(F32)
    for ref in refs[1:]:
        value = value + ref[...].astype(F32)
    return value


def to_lanes(rows, elems, sides):
    return jnp.concatenate([rows[elems * k : elems * (k + 1)] for k in range(sides)], axis=1)


def to_rows(lanes, sides, width):
    return jnp.concatenate([lanes[:, width * k : width * (k + 1)] for k in range(sides)], axis=0)


def spread(spread_hits, values):
    high = values.astype(HALF)
    low = (values - high.astype(F32)).astype(HALF)
    return contract(spread_hits, high, 1, 0) + contract(spread_hits, low, 1, 0)


def hit_rows(ids, rows, group_faces, border, groups):
    group = lax.axis_index("elem")
    own = ids - group * group_faces
    low = ids - lax.rem(group + groups - 1, groups) * group_faces
    place = jnp.where((own >= 0) & (own < group_faces), own, low + group_faces)
    place = jnp.where(ids < 0, -1, place)
    elems, sides = ids.shape
    lane = lax.broadcasted_iota(jnp.int32, (elems, rows), 1)
    return jnp.concatenate(
        [(place[:, k : k + 1] == lane).astype(F32) for k in range(sides)], axis=0
    )


def masked(rows, element):
    index = lax.broadcasted_iota(jnp.int32, rows.shape, 0)
    return jnp.where(index == element, rows, 0.0).astype(HALF)


def load_kernel(dims, *refs):
    groups, elems, sides, width, group_faces, border = dims
    sources, (local_ref, packet_ref, ids_ref, inverse, down, up) = refs[:7], refs[7:13]
    residual, ids, residual_rows, stab_rows, sems = refs[13:]
    rows = group_faces + border
    lines = 2 * elems

    def fetch(index, target, at, count, sem):
        piece = pl.ds(at, count)
        copy = pltpu.make_async_copy(sources[index].at[piece], target.at[piece], sems.at[sem])
        copy.start()
        return copy

    inverse_hbm, down_hbm, up_hbm, residual_hbm, ids_hbm, residual_rows_hbm, stab_rows_hbm = range(7)
    own_faces = residual_rows.shape[0]
    first = [fetch(residual_hbm, residual, 0, elems, 0), fetch(inverse_hbm, inverse, 0, elems, 1)]
    down_copy = fetch(down_hbm, down, 0, elems, 2)
    small = [
        fetch(ids_hbm, ids, 0, elems, 3),
        fetch(residual_rows_hbm, residual_rows, 0, own_faces, 4),
        fetch(stab_rows_hbm, stab_rows, 0, own_faces, 5),
    ]
    up_copy = fetch(up_hbm, up, 0, elems, 6)
    for copy in first:
        copy.wait()
    source = residual[...].astype(F32)
    source = jnp.concatenate([source, jnp.zeros_like(source)], axis=0)
    local = add_up([contract(masked(source, e), inverse[e], 1, 1) for e in range(elems)])
    local_ref[...] = local
    for copy in small:
        copy.wait()
    ids_ref[...] = jnp.full((lines, sides), -1, jnp.int32)
    ids_ref[:elems] = ids[...]
    hits = hit_rows(ids_ref[...], rows, group_faces, border, groups)
    spread_hits = hits.T.astype(HALF)
    place = lax.axis_index("face") * own_faces
    blank = jnp.zeros((rows - own_faces, width), F32)
    right = pltpu.roll(jnp.concatenate([residual_rows[...], blank], axis=0), place, 0)
    scale = pltpu.roll(jnp.concatenate([stab_rows[...], blank], axis=0), place, 0)
    packet_ref[:lines, 2 * width :] = ids_ref[...].astype(F32)
    down_copy.wait()
    load = [contract(masked(local, e), down[e], 1, 0) for e in range(elems)]
    sums = spread(spread_hits, to_rows(add_up(load), sides, width))
    packet_ref[:, : 2 * width] = jnp.concatenate([right - sums, scale], axis=1)
    up_copy.wait()


def join_kernel(border, width, packet, mate, sums_ref, first_ref, second_ref):
    sums = packet[:, : 2 * width] + mate[:, : 2 * width]
    sums_ref[...] = sums
    deal(sums, border, first_ref, second_ref)


def pack_kernel(chip_faces, sums, sent_ref):
    width = sums.shape[1] // 2
    half = width // 2
    chip = lax.axis_index("face") // CORES
    scale = pltpu.roll(sums[:, width:], back(chip * chip_faces, sums.shape[0]), 0)[:chip_faces]
    sent_ref[...] = jnp.zeros(sent_ref.shape, F32)
    sent_ref[:, :width] = sums[:, :width]
    sent_ref[:chip_faces, width:] = scale[:, :half]
    sent_ref[chip_faces : 2 * chip_faces, width:] = scale[:, half:]


def back(shift, rows):
    return lax.rem(rows - shift, rows)


def deal(sums, border, first_ref, second_ref):
    even = lax.rem(lax.axis_index("elem"), 2) == 0
    upper, lower = sums[:border], sums[sums.shape[0] - border :]
    kind = first_ref.dtype
    first_ref[:border] = jnp.where(even, upper, lower).astype(kind)
    if first_ref.shape[0] > border:
        first_ref[border:] = sums[: first_ref.shape[0] - border].astype(kind)
    second_ref[:border] = jnp.where(even, lower, upper).astype(kind)
    if second_ref.shape[0] > border:
        second_ref[border:] = sums[: second_ref.shape[0] - border].astype(kind)


def hits_kernel(dims, ids, mate, hits_ref, spread_ref):
    groups, elems, sides, width, group_faces, border = dims
    far = mate[:elems, 2 * width :].astype(jnp.int32)
    both = jnp.concatenate([ids[:elems], far], axis=0)
    hits = hit_rows(both, group_faces + border, group_faces, border, groups)
    hits_ref[...] = hits.astype(HALF)
    spread_ref[...] = hits.T.astype(HALF)


def whole(parts, border):
    own, first, second, (mate,) = parts
    even = lax.rem(lax.axis_index("elem"), 2) == 0
    blocks = mate[...].astype(F32)
    a, b = add_up(first)[:border], add_up(second)[:border]
    for n in range(len(first)):
        a = a + blocks[n * border : (n + 1) * border]
        b = b + blocks[(len(first) + n) * border : (len(first) + n + 1) * border]
    upper, lower = jnp.where(even, a, b), jnp.where(even, b, a)
    sums = add_up(own)
    last = sums.shape[0] - border
    return jnp.concatenate([sums[:border] + upper, sums[border:last], sums[last:] + lower], axis=0)


def image(trace_now, hits, spread_hits, schur, sides):
    pieces = [block[e] for block in schur for e in range(block.shape[0])]
    picked = contract(hits[...], trace_now.astype(HALF), 1, 0)
    lam = to_lanes(picked, len(pieces), sides)
    terms = add_up([contract(masked(lam, e), block, 1, 0) for e, block in enumerate(pieces)])
    return contract(spread_hits[...], to_rows(terms, sides, trace_now.shape[1]).astype(HALF), 1, 0)


def own_kernel(chip_faces, sums, *refs):
    *across, total_ref = refs
    rows, width = sums.shape[0], sums.shape[1] // 2
    chip = lax.axis_index("face") // CORES
    chips = len(across) + 1
    total = sums[...]
    for n, block in enumerate(across):
        packed = block[...]
        pair = [packed[chip_faces * k : chip_faces * (k + 1), width:] for k in range(2)]
        scale = jnp.concatenate(pair, axis=1)
        scale = jnp.concatenate([scale, jnp.zeros((rows - chip_faces, width), F32)], axis=0)
        scale = pltpu.roll(scale, lax.rem(chip + chips - n - 1, chips) * chip_faces, 0)
        total = total + jnp.concatenate([packed[:, :width], scale], axis=1)
    total_ref[...] = total


def first_kernel(counts, border, sides, *refs):
    parts, rest = split(counts, refs)
    hits, spread_hits, *schur, right_ref, scale_ref, sums_ref, sent_ref, first_ref, second_ref = rest
    both = whole(parts, border)
    width = both.shape[1] // 2
    right = both[:, :width]
    scale = 1.0 / both[:, width:]
    right_ref[...] = right
    scale_ref[...] = scale
    sums = image(right * scale, hits, spread_hits, schur, sides)
    sums_ref[...] = sums
    sent_ref[...] = sums.astype(HALF)
    deal(sums, border, first_ref, second_ref)


def step_kernel(counts, border, sides, *refs):
    parts, rest = split(counts, refs)
    right, scale, hits, spread_hits, *schur, sums_ref, sent_ref, first_ref, second_ref = rest
    trace_now = (whole(parts, border) + right[...]) * scale[...]
    sums = image(trace_now, hits, spread_hits, schur, sides)
    sums_ref[...] = sums
    sent_ref[...] = sums.astype(HALF)
    deal(sums, border, first_ref, second_ref)


def turn_kernel(couple, after, turned_ref):
    for e in range(couple.shape[0]):
        turned_ref[e] = couple[e].T


def last_kernel(counts, border, sides, *refs):
    parts, rest = split(counts, refs)
    right, scale, hits, couple, local, trace_ref, vol_ref = rest
    trace_now = (whole(parts, border) + right[...]) * scale[...]
    own_faces = trace_ref.shape[0]
    place = lax.axis_index("face") * own_faces
    rows = trace_now.shape[0]
    trace_ref[...] = pltpu.roll(trace_now, back(place, rows), 0)[:own_faces]
    elems = couple.shape[0]
    picked = contract(hits[...], trace_now.astype(HALF), 1, 0)
    lam = to_lanes(picked, 2 * elems, sides)
    value = local[...]
    for e in range(elems):
        value = value - contract(masked(lam, e), couple[e], 1, 0)
    vol_ref[...] = value[:elems]


def split(counts, refs):
    parts = []
    for count in counts:
        parts.append(refs[:count])
        refs = refs[count:]
    return parts, refs


def local(
    vol_inverse,
    vol_from_trace,
    trace_from_vol,
    vol_residual,
    face_ids,
    trace_residual,
    stabilization,
):
    groups = lax.axis_size("elem")
    members = lax.axis_size("face")
    chips = members // CORES
    elems, sides = face_ids.shape
    volume = vol_residual.shape[1]
    own_faces, width = trace_residual.shape
    group_faces = own_faces * members
    border = elems * members
    rows = group_faces + border
    slots = 2 * elems * sides
    trace = sides * width
    dims = (groups, elems, sides, width, group_faces, border)

    def swap_core(block):
        return lax.ppermute(block, AXES, other_core(groups, chips))

    def exchange(part, sent, to_first, to_second):
        straight = [
            [shift + core for core in range(CORES)] for shift in range(0, chips, CORES)
        ]
        second = [lax.ppermute(to_second, AXES, partners(groups, chips, 1, s)) for s in straight]
        first = [lax.ppermute(to_first, AXES, partners(groups, chips, 0, s)) for s in straight]
        own = [part] + [
            lax.ppermute(sent, AXES, along_x(groups, chips, shift)) for shift in range(1, chips)
        ]
        mate = swap_core(jnp.concatenate([block[:border] for block in (*first, *second)]))
        return own, first, second, [mate]

    down = jnp.swapaxes(trace_from_vol, 1, 2)
    large = (vol_inverse, down, vol_from_trace)
    small = (vol_residual, face_ids, trace_residual, stabilization)
    local_part, packet, ids, inverse, down, up = call(
        functools.partial(load_kernel, dims),
        [
            ((2 * elems, volume), F32),
            ((rows, 2 * width + sides), F32),
            ((2 * elems, sides), jnp.int32),
            *((array.shape, array.dtype) for array in large),
        ],
        *large, *small,
        stay=7,
        scratch=[
            *(pltpu.VMEM(array.shape, array.dtype) for array in small),
            pltpu.SemaphoreType.DMA((7,)),
        ],
    )
    mate = swap_core(packet)
    couple = jnp.einsum(
        "evk,ekt->evt", inverse, up, preferred_element_type=F32
    ).astype(HALF)
    couple, mate = lax.optimization_barrier((couple, mate))
    chip_faces = CORES * own_faces
    sums, to_first, to_second = call(
        functools.partial(join_kernel, border, width),
        [
            ((rows, 2 * width), F32),
            ((border + 16, 2 * width), F32),
            ((border, 2 * width), F32),
        ],
        packet, mate,
    )
    couple, sums = lax.optimization_barrier((couple, sums))
    schur_own = jnp.einsum("evs,evt->est", couple, down, preferred_element_type=F32).astype(HALF)
    schur_mate = swap_core(schur_own)
    hits, spread_hits = call(
        functools.partial(hits_kernel, dims),
        [((slots, rows), HALF), ((rows, slots), HALF)],
        ids, mate,
        cost=WAIT,
    )

    def counted(kernel, parts):
        return functools.partial(kernel, tuple(len(part) for part in parts), border, sides)

    def flat(parts):
        return [ref for part in parts for ref in part]

    dealt = [
        ((rows, width), F32),
        ((rows, width), HALF),
        ((border, width), HALF),
        ((2 * border, width), HALF),
    ]
    sums, schur_own = lax.optimization_barrier((sums, schur_own))
    (sent,) = call(
        functools.partial(pack_kernel, chip_faces), [((rows, width + width // 2), F32)], sums
    )
    (_, *across), *rest = exchange(sums, sent, to_first, to_second)
    own = call(
        functools.partial(own_kernel, chip_faces), [((rows, 2 * width), F32)], sums, *across
    )
    parts = own, *rest
    right, scale, *out = call(
        counted(first_kernel, parts),
        [((rows, width), F32)] * 2 + dealt,
        *flat(parts), hits, spread_hits, schur_own, schur_mate,
    )
    (turned,) = call(
        turn_kernel, [((elems, trace, volume), HALF)], couple, right,
        cost=pl.CostEstimate(flops=10**9, bytes_accessed=0, transcendentals=0),
    )
    for _ in range(SWEEPS - 2):
        parts = exchange(*out)
        out = call(
            counted(step_kernel, parts), dealt,
            *flat(parts), right, scale, hits, spread_hits, schur_own, schur_mate,
        )
    parts = exchange(*out)
    trace_update, vol_update = call(
        counted(last_kernel, parts),
        [((own_faces, width), F32), ((elems, volume), F32)],
        *flat(parts), right, scale, hits, turned, local_part,
    )
    return trace_update, vol_update


def solution(mesh):
    in_specs = (
        P(AXES, None, None),
        P(AXES, None, None),
        P(AXES, None, None),
        P(AXES, None),
        P(AXES, None),
        P(AXES, None),
        P(AXES, None),
    )
    out_specs = (P(AXES, None), P(AXES, None))
    return jax.shard_map(local, mesh=mesh, in_specs=in_specs, out_specs=out_specs, check_vma=False)
```

```python
import functools

import jax
import jax.numpy as jnp
from jax import lax
from jax.experimental import pallas as pl
from jax.experimental.pallas import tpu as pltpu
from jax.sharding import PartitionSpec as P

SWEEPS = 5
WAIT = pl.CostEstimate(flops=70 * 10**9, bytes_accessed=0, transcendentals=0)
AXES = ("elem", "face")
CORES = 2
F32 = jnp.float32
HALF = jnp.bfloat16
VMEM = pl.BlockSpec(memory_space=pltpu.VMEM)
HBM = pl.BlockSpec(memory_space=pltpu.HBM)


def partners(groups, chips, offset, shifts):
    route = []
    for group in range(groups):
        side = 1 if (group - offset) % 2 == 0 else -1
        other = (group + side) % groups
        for chip in range(chips):
            for core in range(CORES):
                target = (chip + side * shifts[core]) % chips
                route.append(
                    (
                        (group * chips + chip) * CORES + core,
                        (other * chips + target) * CORES + core,
                    )
                )
    return route


def along_x(groups, chips, shift):
    return [
        (
            (group * chips + chip) * CORES + core,
            (group * chips + (chip + shift) % chips) * CORES + (core + 1) % CORES,
        )
        for group in range(groups)
        for chip in range(chips)
        for core in range(CORES)
    ]


def other_core(groups, chips):
    return [
        (chip * CORES + core, chip * CORES + 1 - core)
        for chip in range(groups * chips)
        for core in range(CORES)
    ]


def call(body, shapes, *args, limit=16, stay=0, scratch=(), cost=None):
    outs = [jax.ShapeDtypeStruct(shape, kind) for shape, kind in shapes]
    args = [
        pltpu.with_memory_space_constraint(arg, pltpu.HBM) if n < stay else arg
        for n, arg in enumerate(args)
    ]
    return pl.pallas_call(
        body,
        out_shape=outs,
        in_specs=[HBM] * stay + [VMEM] * (len(args) - stay),
        out_specs=[VMEM] * len(outs),
        scratch_shapes=list(scratch),
        cost_estimate=cost,
        compiler_params=pltpu.CompilerParams(vmem_limit_bytes=limit * 2**20),
    )(*args)


def contract(left, right, left_dim, right_dim):
    return lax.dot_general(
        left, right, (((left_dim,), (right_dim,)), ((), ())), preferred_element_type=F32
    )


def add_up(refs):
    value = refs[0][...].astype(F32)
    for ref in refs[1:]:
        value = value + ref[...].astype(F32)
    return value


def to_lanes(rows, elems, sides):
    return jnp.concatenate([rows[elems * k : elems * (k + 1)] for k in range(sides)], axis=1)


def to_rows(lanes, sides, width):
    return jnp.concatenate([lanes[:, width * k : width * (k + 1)] for k in range(sides)], axis=0)


def spread(spread_hits, values):
    high = values.astype(HALF)
    low = (values - high.astype(F32)).astype(HALF)
    return contract(spread_hits, high, 1, 0) + contract(spread_hits, low, 1, 0)


def hit_rows(ids, rows, group_faces, border, groups):
    group = lax.axis_index("elem")
    own = ids - group * group_faces
    low = ids - lax.rem(group + groups - 1, groups) * group_faces
    place = jnp.where((own >= 0) & (own < group_faces), own, low + group_faces)
    place = jnp.where(ids < 0, -1, place)
    elems, sides = ids.shape
    lane = lax.broadcasted_iota(jnp.int32, (elems, rows), 1)
    return jnp.concatenate(
        [(place[:, k : k + 1] == lane).astype(F32) for k in range(sides)], axis=0
    )


def masked(rows, element):
    index = lax.broadcasted_iota(jnp.int32, rows.shape, 0)
    return jnp.where(index == element, rows, 0.0).astype(HALF)


def load_kernel(dims, *refs):
    groups, elems, sides, width, group_faces, border = dims
    sources, (local_ref, packet_ref, ids_ref, inverse, down, up) = refs[:7], refs[7:13]
    residual, ids, residual_rows, stab_rows, sems = refs[13:]
    rows = group_faces + border
    lines = 2 * elems

    def fetch(index, target, at, count, sem):
        piece = pl.ds(at, count)
        copy = pltpu.make_async_copy(sources[index].at[piece], target.at[piece], sems.at[sem])
        copy.start()
        return copy

    inverse_hbm, down_hbm, up_hbm, residual_hbm, ids_hbm, residual_rows_hbm, stab_rows_hbm = range(7)
    own_faces = residual_rows.shape[0]
    first = [fetch(residual_hbm, residual, 0, elems, 0), fetch(inverse_hbm, inverse, 0, elems, 1)]
    down_copy = fetch(down_hbm, down, 0, elems, 2)
    small = [
        fetch(ids_hbm, ids, 0, elems, 3),
        fetch(residual_rows_hbm, residual_rows, 0, own_faces, 4),
        fetch(stab_rows_hbm, stab_rows, 0, own_faces, 5),
    ]
    up_copy = fetch(up_hbm, up, 0, elems, 6)
    for copy in first:
        copy.wait()
    source = residual[...].astype(F32)
    source = jnp.concatenate([source, jnp.zeros_like(source)], axis=0)
    local = add_up([contract(masked(source, e), inverse[e], 1, 1) for e in range(elems)])
    local_ref[...] = local
    for copy in small:
        copy.wait()
    ids_ref[...] = jnp.full((lines, sides), -1, jnp.int32)
    ids_ref[:elems] = ids[...]
    hits = hit_rows(ids_ref[...], rows, group_faces, border, groups)
    spread_hits = hits.T.astype(HALF)
    place = lax.axis_index("face") * own_faces
    blank = jnp.zeros((rows - own_faces, width), F32)
    right = pltpu.roll(jnp.concatenate([residual_rows[...], blank], axis=0), place, 0)
    scale = pltpu.roll(jnp.concatenate([stab_rows[...], blank], axis=0), place, 0)
    packet_ref[:lines, 2 * width :] = ids_ref[...].astype(F32)
    down_copy.wait()
    load = [contract(masked(local, e), down[e], 1, 0) for e in range(elems)]
    sums = spread(spread_hits, to_rows(add_up(load), sides, width))
    packet_ref[:, : 2 * width] = jnp.concatenate([right - sums, scale], axis=1)
    up_copy.wait()


def join_kernel(border, width, packet, mate, sums_ref, first_ref, second_ref):
    sums = packet[:, : 2 * width] + mate[:, : 2 * width]
    sums_ref[...] = sums
    deal(sums, border, first_ref, second_ref)


def pack_kernel(chip_faces, sums, sent_ref):
    width = sums.shape[1] // 2
    half = width // 2
    chip = lax.axis_index("face") // CORES
    scale = pltpu.roll(sums[:, width:], back(chip * chip_faces, sums.shape[0]), 0)[:chip_faces]
    sent_ref[...] = jnp.zeros(sent_ref.shape, F32)
    sent_ref[:, :width] = sums[:, :width]
    sent_ref[:chip_faces, width:] = scale[:, :half]
    sent_ref[chip_faces : 2 * chip_faces, width:] = scale[:, half:]


def back(shift, rows):
    return lax.rem(rows - shift, rows)


def deal(sums, border, first_ref, second_ref):
    even = lax.rem(lax.axis_index("elem"), 2) == 0
    upper, lower = sums[:border], sums[sums.shape[0] - border :]
    kind = first_ref.dtype
    first_ref[:border] = jnp.where(even, upper, lower).astype(kind)
    if first_ref.shape[0] > border:
        first_ref[border:] = sums[: first_ref.shape[0] - border].astype(kind)
    second_ref[:border] = jnp.where(even, lower, upper).astype(kind)
    if second_ref.shape[0] > border:
        second_ref[border:] = sums[: second_ref.shape[0] - border].astype(kind)


def hits_kernel(dims, ids, mate, hits_ref, spread_ref):
    groups, elems, sides, width, group_faces, border = dims
    far = mate[:elems, 2 * width :].astype(jnp.int32)
    both = jnp.concatenate([ids[:elems], far], axis=0)
    hits = hit_rows(both, group_faces + border, group_faces, border, groups)
    hits_ref[...] = hits.astype(HALF)
    spread_ref[...] = hits.T.astype(HALF)


def whole(parts, border):
    own, first, second, (mate,) = parts
    even = lax.rem(lax.axis_index("elem"), 2) == 0
    blocks = mate[...].astype(F32)
    a, b = add_up(first)[:border], add_up(second)[:border]
    for n in range(len(first)):
        a = a + blocks[n * border : (n + 1) * border]
        b = b + blocks[(len(first) + n) * border : (len(first) + n + 1) * border]
    upper, lower = jnp.where(even, a, b), jnp.where(even, b, a)
    sums = add_up(own)
    last = sums.shape[0] - border
    return jnp.concatenate([sums[:border] + upper, sums[border:last], sums[last:] + lower], axis=0)


def known_kernel(counts, border, *refs):
    (own, first, second), (right, known_ref) = split(counts, refs)
    even = lax.rem(lax.axis_index("elem"), 2) == 0
    a, b = add_up(first)[:border], add_up(second)[:border]
    upper, lower = jnp.where(even, a, b), jnp.where(even, b, a)
    last = known_ref.shape[0] - border
    known_ref[...] = add_up(own) + right[...]
    known_ref[:border] += upper
    known_ref[last:] += lower


def completed(known, mate, border):
    even = lax.rem(lax.axis_index("elem"), 2) == 0
    half = mate.shape[0] // 2
    a, b = (
        add_up([mate.at[pl.ds(at + n * border, border)] for n in range(half // border)])
        for at in (0, half)
    )
    upper, lower = jnp.where(even, a, b), jnp.where(even, b, a)
    sums = known[...]
    last = sums.shape[0] - border
    return jnp.concatenate([sums[:border] + upper, sums[border:last], sums[last:] + lower], axis=0)


def image(trace_now, hits, spread_hits, schur, sides):
    pieces = [block[e] for block in schur for e in range(block.shape[0])]
    picked = contract(hits[...], trace_now.astype(HALF), 1, 0)
    lam = to_lanes(picked, len(pieces), sides)
    terms = add_up([contract(masked(lam, e), block, 1, 0) for e, block in enumerate(pieces)])
    return contract(spread_hits[...], to_rows(terms, sides, trace_now.shape[1]).astype(HALF), 1, 0)


def own_kernel(chip_faces, sums, *refs):
    *across, total_ref = refs
    rows, width = sums.shape[0], sums.shape[1] // 2
    chip = lax.axis_index("face") // CORES
    chips = len(across) + 1
    total = sums[...]
    for n, block in enumerate(across):
        packed = block[...]
        pair = [packed[chip_faces * k : chip_faces * (k + 1), width:] for k in range(2)]
        scale = jnp.concatenate(pair, axis=1)
        scale = jnp.concatenate([scale, jnp.zeros((rows - chip_faces, width), F32)], axis=0)
        scale = pltpu.roll(scale, lax.rem(chip + chips - n - 1, chips) * chip_faces, 0)
        total = total + jnp.concatenate([packed[:, :width], scale], axis=1)
    total_ref[...] = total


def first_kernel(counts, border, sides, *refs):
    parts, rest = split(counts, refs)
    hits, spread_hits, *schur, right_ref, scale_ref, sums_ref, sent_ref, first_ref, second_ref = rest
    both = whole(parts, border)
    width = both.shape[1] // 2
    right = both[:, :width]
    scale = 1.0 / both[:, width:]
    right_ref[...] = right
    scale_ref[...] = scale
    sums = image(right * scale, hits, spread_hits, schur, sides)
    sums_ref[...] = sums
    sent_ref[...] = sums.astype(HALF)
    deal(sums, border, first_ref, second_ref)


def step_kernel(border, sides, known, mate, *rest):
    scale, hits, spread_hits, *schur, sums_ref, sent_ref, first_ref, second_ref = rest
    trace_now = completed(known, mate, border) * scale[...]
    sums = image(trace_now, hits, spread_hits, schur, sides)
    sums_ref[...] = sums
    sent_ref[...] = sums.astype(HALF)
    deal(sums, border, first_ref, second_ref)


def turn_kernel(couple, after, turned_ref):
    for e in range(couple.shape[0]):
        turned_ref[e] = couple[e].T


def last_kernel(border, sides, known, mate, *rest):
    scale, hits, couple, local, trace_ref, vol_ref = rest
    trace_now = completed(known, mate, border) * scale[...]
    own_faces = trace_ref.shape[0]
    place = lax.axis_index("face") * own_faces
    rows = trace_now.shape[0]
    trace_ref[...] = pltpu.roll(trace_now, back(place, rows), 0)[:own_faces]
    elems = couple.shape[0]
    picked = contract(hits[...], trace_now.astype(HALF), 1, 0)
    lam = to_lanes(picked, 2 * elems, sides)
    value = local[...]
    for e in range(elems):
        value = value - contract(masked(lam, e), couple[e], 1, 0)
    vol_ref[...] = value[:elems]


def split(counts, refs):
    parts = []
    for count in counts:
        parts.append(refs[:count])
        refs = refs[count:]
    return parts, refs


def local(
    vol_inverse,
    vol_from_trace,
    trace_from_vol,
    vol_residual,
    face_ids,
    trace_residual,
    stabilization,
):
    groups = lax.axis_size("elem")
    members = lax.axis_size("face")
    chips = members // CORES
    elems, sides = face_ids.shape
    volume = vol_residual.shape[1]
    own_faces, width = trace_residual.shape
    group_faces = own_faces * members
    border = elems * members
    rows = group_faces + border
    slots = 2 * elems * sides
    trace = sides * width
    dims = (groups, elems, sides, width, group_faces, border)

    def swap_core(block):
        return lax.ppermute(block, AXES, other_core(groups, chips))

    def exchange(part, sent, to_first, to_second):
        straight = [
            [shift + core for core in range(CORES)] for shift in range(0, chips, CORES)
        ]
        second = [lax.ppermute(to_second, AXES, partners(groups, chips, 1, s)) for s in straight]
        first = [lax.ppermute(to_first, AXES, partners(groups, chips, 0, s)) for s in straight]
        own = [part] + [
            lax.ppermute(sent, AXES, along_x(groups, chips, shift)) for shift in range(1, chips)
        ]
        mate = swap_core(jnp.concatenate([block[:border] for block in (*first, *second)]))
        return own, first, second, [mate]

    down = jnp.swapaxes(trace_from_vol, 1, 2)
    large = (vol_inverse, down, vol_from_trace)
    small = (vol_residual, face_ids, trace_residual, stabilization)
    local_part, packet, ids, inverse, down, up = call(
        functools.partial(load_kernel, dims),
        [
            ((2 * elems, volume), F32),
            ((rows, 2 * width + sides), F32),
            ((2 * elems, sides), jnp.int32),
            *((array.shape, array.dtype) for array in large),
        ],
        *large, *small,
        stay=7,
        scratch=[
            *(pltpu.VMEM(array.shape, array.dtype) for array in small),
            pltpu.SemaphoreType.DMA((7,)),
        ],
    )
    mate = swap_core(packet)
    couple = jnp.einsum(
        "evk,ekt->evt", inverse, up, preferred_element_type=F32
    ).astype(HALF)
    couple, mate = lax.optimization_barrier((couple, mate))
    chip_faces = CORES * own_faces
    sums, to_first, to_second = call(
        functools.partial(join_kernel, border, width),
        [
            ((rows, 2 * width), F32),
            ((border + 16, 2 * width), F32),
            ((border, 2 * width), F32),
        ],
        packet, mate,
    )
    couple, sums = lax.optimization_barrier((couple, sums))
    schur_own = jnp.einsum("evs,evt->est", couple, down, preferred_element_type=F32).astype(HALF)
    schur_mate = swap_core(schur_own)
    hits, spread_hits = call(
        functools.partial(hits_kernel, dims),
        [((slots, rows), HALF), ((rows, slots), HALF)],
        ids, mate,
        cost=WAIT,
    )

    def counted(kernel, parts):
        return functools.partial(kernel, tuple(len(part) for part in parts), border, sides)

    def flat(parts):
        return [ref for part in parts for ref in part]

    dealt = [
        ((rows, width), F32),
        ((rows, width), HALF),
        ((border, width), HALF),
        ((2 * border, width), HALF),
    ]
    sums, schur_own = lax.optimization_barrier((sums, schur_own))
    (sent,) = call(
        functools.partial(pack_kernel, chip_faces), [((rows, width + width // 2), F32)], sums
    )
    (_, *across), *rest = exchange(sums, sent, to_first, to_second)
    own = call(
        functools.partial(own_kernel, chip_faces), [((rows, 2 * width), F32)], sums, *across
    )
    parts = own, *rest
    right, scale, *out = call(
        counted(first_kernel, parts),
        [((rows, width), F32)] * 2 + dealt,
        *flat(parts), hits, spread_hits, schur_own, schur_mate,
    )
    (turned,) = call(
        turn_kernel, [((elems, trace, volume), HALF)], couple, right,
        cost=pl.CostEstimate(flops=10**9, bytes_accessed=0, transcendentals=0),
    )

    def gathered(*sent_parts):
        *parts, (mate,) = exchange(*sent_parts)
        counts = tuple(len(part) for part in parts)
        (known,) = call(
            functools.partial(known_kernel, counts, border), [((rows, width), F32)],
            *flat(parts), right,
        )
        return known, mate

    for _ in range(SWEEPS - 2):
        out = call(
            functools.partial(step_kernel, border, sides), dealt,
            *gathered(*out), scale, hits, spread_hits, schur_own, schur_mate,
        )
    trace_update, vol_update = call(
        functools.partial(last_kernel, border, sides),
        [((own_faces, width), F32), ((elems, volume), F32)],
        *gathered(*out), scale, hits, turned, local_part,
    )
    return trace_update, vol_update


def solution(mesh):
    in_specs = (
        P(AXES, None, None),
        P(AXES, None, None),
        P(AXES, None, None),
        P(AXES, None),
        P(AXES, None),
        P(AXES, None),
        P(AXES, None),
    )
    out_specs = (P(AXES, None), P(AXES, None))
    return jax.shard_map(local, mesh=mesh, in_specs=in_specs, out_specs=out_specs, check_vma=False)
```
